256 devices in a mesh: space: 32 (over x, y, core), mem: 8 (over z).
Axes of the slice: x: 4, y: 4, z: 8, core: 2. Of those that a mesh axis runs over, the one named last changes fastest.
Arguments:
- fields: bfloat16 [64, 64, 64, 384], P('mem', None, 'space'), may hold values from -6 to 6
- w_qkv: bfloat16 [9, 192, 64], replicated, may hold values from -1 to 1
- w_out: bfloat16 [9, 64, 64], replicated, may hold values from -0.25 to 0.25
Outputs:
- mixed: bfloat16 [64, 64, 64, 384], P('mem', None, 'space')
The draws below stay inside these ranges and needn't reach their ends.
All inputs are finite; a program needn't handle non-finite values.
Results may differ from the reference program's by a relative error of at most 0.007.
Values may be sent and summed in bfloat16 or wider, within the bound.
No kernel may reach another device: no remote copies, remote signals or barrier semaphores. Data moves between devices by JAX's collectives and lax.ppermute only.
A program may use at most 64 MiB of HBM per device.

```python
import math
import jax
import jax.numpy as jnp
from jax import lax

C = 64
HEADS = 8
HD = 8
LON = 384
MEMBERS = 64
NLAT = 64


def draw_fields(key, part):
    key = jax.random.fold_in(key, 7)
    key_own = jax.random.fold_in(key, 0)
    lat_frac = jnp.arange(NLAT, dtype=jnp.float32).reshape(1, 1, NLAT, 1) / max(NLAT - 1, 1)
    amplitude = 0.8 * jnp.power(3.0, 0.5 * lat_frac)
    drawn = amplitude * jax.random.truncated_normal(key_own, -4.0, 4.0, (MEMBERS, C, NLAT, LON), jnp.float32)
    return drawn.astype(jnp.bfloat16)


def draw_w_qkv(key, part):
    key = jax.random.fold_in(key, 11)
    key_query, key_key, key_sign, key_value = jax.random.split(key, 4)
    spread = 1.0 / math.sqrt(9 * C)
    half_shape = (9, C // 2, C)
    query_base = spread * jax.random.truncated_normal(key_query, -4.0, 4.0, half_shape, jnp.float32)
    key_base = spread * jax.random.truncated_normal(key_key, -4.0, 4.0, half_shape, jnp.float32)
    signs = 2.0 * jax.random.bernoulli(key_sign, 0.5, half_shape).astype(jnp.float32) - 1.0
    query_part = jnp.stack([query_base, query_base * signs], axis=2).reshape(9, C, C)
    key_part = jnp.stack([key_base, -(key_base * signs)], axis=2).reshape(9, C, C)
    value_part = spread * jax.random.truncated_normal(key_value, -4.0, 4.0, (9, C, C), jnp.float32)
    return jnp.concatenate([query_part, key_part, value_part], axis=1).astype(jnp.bfloat16)


def bell_draw(key, shape, scale, limit, held_as=jnp.bfloat16):
    array = jax.random.normal(key, shape, jnp.float32) * scale
    return jnp.minimum(jnp.maximum(array, -limit), limit).astype(held_as)


def setup_inputs(seed: int = 0) -> dict:
    streams_of = jax.random.split(jax.random.key(seed), 4)
    return {
        "fields": draw_fields(jax.random.fold_in(streams_of[3], 71), 0),
        "w_qkv": draw_w_qkv(jax.random.fold_in(streams_of[3], 71), 0),
        "w_out": bell_draw(streams_of[2], (9, C, C), (9 * C) ** -0.5, 0.25),
    }


def pad_member(member_field):
    return jnp.pad(member_field, ((0, 0), (1, 1), (1, 1)))

def member_conv(padded, weights):
    summed = jnp.zeros((weights.shape[1], NLAT * LON), jnp.float32)
    for lat_shift in range(3):
        for lon_shift in range(3):
            shifted = padded[:, lat_shift:lat_shift + NLAT, lon_shift:lon_shift + LON].reshape(C, NLAT * LON)
            summed = summed + jnp.dot(weights[3 * lat_shift + lon_shift], shifted, preferred_element_type=jnp.float32)
    return summed.reshape(weights.shape[1], NLAT, LON)

def reference(fields, w_qkv, w_out):
    projections = lax.map(lambda member_field: member_conv(pad_member(member_field), w_qkv).astype(jnp.bfloat16), fields)
    score_scale = 1.0 / math.sqrt(HD * NLAT * LON)

    def one_head(head):
        queries = lax.dynamic_slice_in_dim(projections, head * HD, HD, 1).astype(jnp.float32)
        key_maps = lax.dynamic_slice_in_dim(projections, C + head * HD, HD, 1).astype(jnp.float32)
        values = lax.dynamic_slice_in_dim(projections, 2 * C + head * HD, HD, 1).astype(jnp.float32)
        scores = jnp.einsum('idyx,jdyx->ij', queries, key_maps, precision=lax.Precision.HIGHEST) * score_scale
        weights = jax.nn.softmax(scores, axis=-1)
        attn = lax.optimization_barrier(weights.astype(jnp.bfloat16)).astype(jnp.float32)
        return jnp.einsum('ij,jdyx->idyx', attn, values, precision=lax.Precision.HIGHEST).astype(jnp.bfloat16)
    per_head = lax.map(one_head, jnp.arange(HEADS, dtype=jnp.int32))
    attended = jnp.transpose(per_head, (1, 0, 2, 3, 4)).reshape(MEMBERS, C, NLAT, LON)

    def finish(member_pair):
        return (member_pair[0].astype(jnp.float32) + member_conv(pad_member(member_pair[1]), w_out)).astype(jnp.bfloat16)
    return lax.map(finish, (fields, attended))
```

```python
import math

import jax
import jax.numpy as jnp
from jax import lax
from jax.experimental import pallas as pl
from jax.experimental.pallas import tpu as pltpu
from jax.sharding import Mesh
from jax.sharding import PartitionSpec as P

C = 64
HEADS = 8
HD = 8
M = 64
ROWS = 2
LANES = ROWS * C
GROUPS = 8
LON = 384
LB = LON // GROUPS
LW = LB + 4
LV = LB + 2
SPACE = ("x", "y", "core")
BF = jnp.bfloat16
F32 = jnp.float32
VMEM_LIMIT = 48 * 1024 * 1024


def place_weights_kernel(w_ref, wo_ref, qk_ref, v_ref, o_ref):
    qk_ref[...] = jnp.zeros(qk_ref.shape, BF)
    v_ref[...] = jnp.zeros(v_ref.shape, BF)
    o_ref[...] = jnp.zeros(o_ref.shape, BF)
    for b in range(3):
        for a in range(3):
            tap = w_ref[3 * a + b]
            for ro in range(2):
                rin = 2 + ro + a - 1
                qk_ref[b, rin * C:(rin + 1) * C, ro * C:(ro + 1) * C] = tap[:, 0:C]
                qk_ref[b, rin * C:(rin + 1) * C, LANES + ro * C:LANES + (ro + 1) * C] = tap[:, C:2 * C]
            for ro in range(4):
                rin = ro + a
                v_ref[b, rin * C:(rin + 1) * C, ro * C:(ro + 1) * C] = tap[:, 2 * C:3 * C]
            for ro in range(2):
                rin = ro + a
                o_ref[b, rin * C:(rin + 1) * C, ro * C:(ro + 1) * C] = wo_ref[3 * a + b]


def place_weights(w_qkv, w_out):
    return pl.pallas_call(
        place_weights_kernel,
        out_shape=(
            jax.ShapeDtypeStruct((3, 6 * C, 4 * C), BF),
            jax.ShapeDtypeStruct((3, 6 * C, 4 * C), BF),
            jax.ShapeDtypeStruct((3, 4 * C, 2 * C), BF),
        ),
        compiler_params=pltpu.CompilerParams(vmem_limit_bytes=VMEM_LIMIT),
        cost_estimate=pl.CostEstimate(flops=0, bytes_accessed=1500000, transcendentals=0),
    )(jnp.swapaxes(w_qkv, 1, 2), jnp.swapaxes(w_out, 1, 2))


def conv_block(prev_ref, own_ref, next_ref, w_ref, start, count):
    total = None
    for b in range(3):
        window = pl.ds(start + b, count)
        x = jnp.concatenate([prev_ref[window], own_ref[window], next_ref[window]], axis=-1)
        part = jnp.dot(x.reshape(count * M, 6 * C), w_ref[b], preferred_element_type=F32)
        total = part if total is None else total + part
    return total


def head_of_lane(lanes):
    lane = lax.broadcasted_iota(jnp.int32, (1, lanes), 1)
    return (lane % C) // HD


def scores_kernel(prev_ref, own_ref, next_ref, w_ref, s_ref, acc_ref):
    acc_ref[...] = jnp.zeros(acc_ref.shape, F32)
    head = head_of_lane(2 * LANES)
    masks = [(head == h).astype(BF) for h in range(HEADS)]
    step = 8

    def chunk(i, carry):
        qk = conv_block(prev_ref, own_ref, next_ref, w_ref, 1 + i * step, step).astype(BF)
        q = qk[:, :LANES].reshape(step, M, LANES)
        k = qk[:, LANES:].reshape(step, M, LANES)
        part = None
        for l in range(0, step, 2):
            q2 = jnp.concatenate([q[l], q[l + 1]], axis=-1)
            k2 = jnp.concatenate([k[l], k[l + 1]], axis=-1)
            qm = jnp.concatenate([q2 * mask for mask in masks], axis=0)
            s = lax.dot_general(qm, k2, (((1,), (1,)), ((), ())), preferred_element_type=F32)
            part = s if part is None else part + s
        acc_ref[...] += part
        return carry

    lax.fori_loop(0, LB // step, chunk, 0)
    for h in range(HEADS):
        lo = acc_ref[h * M:h * M + M // 2]
        hi = acc_ref[h * M + M // 2:(h + 1) * M]
        s_ref[h] = jnp.concatenate([lo, hi], axis=-1)


def partial_scores(prev, own, after, w_qk):
    return pl.pallas_call(
        scores_kernel,
        out_shape=jax.ShapeDtypeStruct((HEADS, M // 2, 2 * M), F32),
        scratch_shapes=[pltpu.VMEM((HEADS * M, M), F32)],
        compiler_params=pltpu.CompilerParams(vmem_limit_bytes=VMEM_LIMIT),
        cost_estimate=pl.CostEstimate(flops=4_000_000_000, bytes_accessed=3000000, transcendentals=0),
    )(prev, own, after, w_qk)


def values_kernel(prev_ref, own_ref, next_ref, w_ref, keep_ref, v_ref):
    step = 10

    def chunk(i, carry):
        v = conv_block(prev_ref, own_ref, next_ref, w_ref, i * step, step)
        v = v.reshape(step, M, 4 * C) * keep_ref[pl.ds(i * step, step)]
        v_ref[pl.ds(i * step, step)] = v.astype(BF)
        return carry

    lax.fori_loop(0, LV // step, chunk, 0)


def value_maps(prev, own, after, w_v, keep):
    return pl.pallas_call(
        values_kernel,
        out_shape=jax.ShapeDtypeStruct((LV, M, 4 * C), BF),
        compiler_params=pltpu.CompilerParams(vmem_limit_bytes=VMEM_LIMIT),
        cost_estimate=pl.CostEstimate(flops=2_000_000_000, bytes_accessed=4000000, transcendentals=0),
    )(prev, own, after, w_v, keep)


def mix_kernel(attn_ref, v_ref, own_ref, w_ref, out_ref, att_ref):
    head = head_of_lane(4 * C)
    masks = [(head == h).astype(BF) for h in range(HEADS)]
    attn = jnp.concatenate(
        [jnp.concatenate([attn_ref[h][:, :M], attn_ref[h][:, M:]], axis=0) for h in range(HEADS)], axis=-1
    )

    def blend(t, carry):
        v = v_ref[t]
        vm = jnp.concatenate([v * mask for mask in masks], axis=0)
        att_ref[t] = jnp.dot(attn, vm, preferred_element_type=F32).astype(BF)
        return carry

    lax.fori_loop(0, LV, blend, 0, unroll=5)
    step = 8

    def chunk(i, carry):
        total = own_ref[pl.ds(i * step + 2, step)].astype(F32).reshape(step * M, LANES)
        for b in range(3):
            x = att_ref[pl.ds(i * step + b, step)].reshape(step * M, 4 * C)
            total = total + jnp.dot(x, w_ref[b], preferred_element_type=F32)
        out_ref[pl.ds(i * step, step)] = total.astype(BF).reshape(step, M, LANES)
        return carry

    lax.fori_loop(0, LB // step, chunk, 0)


def mix(attn, v, own, w_o):
    return pl.pallas_call(
        mix_kernel,
        out_shape=jax.ShapeDtypeStruct((LB, M, LANES), BF),
        scratch_shapes=[pltpu.VMEM((LV, M, 4 * C), BF)],
        compiler_params=pltpu.CompilerParams(vmem_limit_bytes=VMEM_LIMIT),
        cost_estimate=pl.CostEstimate(flops=4_000_000_000, bytes_accessed=4000000, transcendentals=0),
    )(attn, v, own, w_o)


def local(fields, w_qkv, w_out):
    members_here = fields.shape[0]
    place = lax.axis_index(SPACE)
    group = lax.axis_index("mem")
    last_place = lax.axis_size(SPACE) - 1
    w_qk, w_v, w_o = place_weights(w_qkv, w_out)

    cells = jnp.transpose(fields, (3, 0, 2, 1)).reshape(LON, members_here, LANES)
    padded = jnp.pad(cells, ((2, 2), (0, 0), (0, 0)))
    windows = jnp.stack([padded[g * LB:g * LB + LW] for g in range(GROUPS)])
    arrived = lax.all_to_all(windows, "mem", split_axis=0, concat_axis=0, tiled=True)
    own = jnp.transpose(arrived, (1, 0, 2, 3)).reshape(LW, M, LANES)
    prev = lax.ppermute(own, SPACE, [(i, i + 1) for i in range(last_place)])
    after = lax.ppermute(own, SPACE, [(i + 1, i) for i in range(last_place)])

    part = partial_scores(prev, own, after, w_qk)
    places = last_place + 1
    part = part.reshape(places, HEADS * M // 2 // places, 2 * M)
    part = lax.all_to_all(part, SPACE, split_axis=0, concat_axis=0, tiled=True).sum(axis=0)
    part = jnp.broadcast_to(part[None], (GROUPS,) + part.shape)
    part = lax.all_to_all(part, "mem", split_axis=0, concat_axis=0, tiled=True)
    row = lax.broadcasted_iota(jnp.int32, (LV, 1, 4 * C), 2) // C
    lon = lax.broadcasted_iota(jnp.int32, (LV, 1, 4 * C), 0)
    outside = (
        ((row == 0) & (place == 0))
        | ((row == 3) & (place == last_place))
        | ((lon == 0) & (group == 0))
        | ((lon == LV - 1) & (group == GROUPS - 1))
    )
    keep = jnp.where(outside, 0.0, 1.0).astype(F32)
    v = value_maps(prev, own, after, w_v, keep)
    part, v = lax.optimization_barrier((part, v))
    total = part.sum(axis=0)
    scale = 1.0 / math.sqrt(HD * ROWS * places * LON)
    attn = jax.nn.softmax((total * scale).reshape(-1, 2, M), axis=-1).astype(BF).reshape(total.shape)
    attn = jnp.broadcast_to(attn[None], (places,) + attn.shape)
    attn = lax.all_to_all(attn, SPACE, split_axis=0, concat_axis=0, tiled=True).reshape(HEADS, M // 2, 2 * M)
    mixed = mix(attn, v, own, w_o)
    mixed = jnp.transpose(mixed.reshape(LB, GROUPS, members_here, LANES), (1, 0, 2, 3))
    back = lax.all_to_all(mixed, "mem", split_axis=0, concat_axis=0, tiled=True)
    back = back.reshape(LON, members_here, ROWS, C)
    return jnp.transpose(back, (1, 3, 2, 0))


def solution(mesh):
    whole = Mesh(mesh.devices.reshape(4, 4, 2, 8), ("x", "y", "core", "mem"))
    return jax.shard_map(
        local,
        mesh=whole,
        in_specs=(P("mem", None, SPACE, None), P(), P()),
        out_specs=P("mem", None, SPACE, None),
        check_vma=False,
    )
```

```python
import math

import jax
import jax.numpy as jnp
from jax import lax
from jax.experimental import pallas as pl
from jax.experimental.pallas import tpu as pltpu
from jax.sharding import Mesh
from jax.sharding import PartitionSpec as P

C = 64
HEADS = 8
HD = 8
M = 64
ROWS = 2
LANES = ROWS * C
GROUPS = 8
LON = 384
LB = LON // GROUPS
LW = LB + 4
LV = LB + 2
HALF = LB // 2
PACK = HALF + 4
SPACE = ("x", "y", "core")
BF = jnp.bfloat16
F32 = jnp.float32
VMEM_LIMIT = 24 * 1024 * 1024


def place_weights_kernel(core_ref, w_ref, wo_ref, qk_ref, near_ref, v_ref, o_ref):
    for ref in (qk_ref, near_ref, v_ref, o_ref):
        ref[...] = jnp.zeros(ref.shape, BF)

    def span(i):
        return slice(i * C, (i + 1) * C)

    def place(core):
        early, late = 1 - core, core
        near = -1 if core == 0 else 2
        far = -2 if core == 0 else 3
        mate = 2 if core == 0 else -2
        in_pair = {mate: 0, mate + 1: 1, 0: 2, 1: 3}
        in_all = {near: 0, far: 1, 0: 2, 1: 3, mate: 4, mate + 1: 5}
        for b in range(3):
            for a in range(3):
                tap = w_ref[3 * a + b]
                for out, part in ((early, 0), (late, 2)):
                    row = out + a - 1
                    if row in in_pair:
                        qk_ref[b, span(in_pair[row]), span(part)] = tap[:, 0:C]
                        qk_ref[b, span(in_pair[row]), span(part + 1)] = tap[:, C:2 * C]
                    else:
                        for half in range(2):
                            near_ref[span(2 * b + half), span(2 * half)] = tap[:, 0:C]
                            near_ref[span(2 * b + half), span(2 * half + 1)] = tap[:, C:2 * C]
                for out in range(-1, 3):
                    v_ref[b, span(in_all[out + a - 1]), span(out + 1)] = tap[:, 2 * C:3 * C]

    pl.when(core_ref[0] == 0)(lambda: place(0))
    pl.when(core_ref[0] == 1)(lambda: place(1))
    for b in range(3):
        for a in range(3):
            for out in range(2):
                o_ref[b, span(out + a), span(out)] = wo_ref[3 * a + b]


def params():
    return pltpu.CompilerParams(vmem_limit_bytes=VMEM_LIMIT)


def cost(flops, moved):
    return pl.CostEstimate(flops=flops, bytes_accessed=moved, transcendentals=0)


def place_weights(core, w_qkv, w_out):
    vmem = pl.BlockSpec(memory_space=pltpu.VMEM)
    return pl.pallas_call(
        place_weights_kernel,
        in_specs=[pl.BlockSpec(memory_space=pltpu.SMEM), vmem, vmem],
        out_shape=(
            jax.ShapeDtypeStruct((3, 4 * C, 4 * C), BF),
            jax.ShapeDtypeStruct((6 * C, 4 * C), BF),
            jax.ShapeDtypeStruct((3, 6 * C, 4 * C), BF),
            jax.ShapeDtypeStruct((3, 4 * C, 2 * C), BF),
        ),
        compiler_params=params(),
        cost_estimate=cost(0, 1500000),
    )(core.reshape(1), jnp.swapaxes(w_qkv, 1, 2), jnp.swapaxes(w_out, 1, 2))


def windows_kernel(rows_ref, out_ref, cells_ref):
    members = rows_ref.shape[0]
    edge = 2 * members
    cells_ref[:edge] = jnp.zeros((edge, LANES), F32)
    cells_ref[edge + LON * members:] = jnp.zeros((edge, LANES), F32)
    for m in range(members):
        cells_ref[pl.ds(edge + m, LON, stride=members)] = rows_ref[m].astype(F32).T
    for g in range(GROUPS):
        start = g * LB * members
        out_ref[g] = cells_ref[start:start + LW * members].astype(BF)


def windows_of(rows):
    members = rows.shape[0]
    return pl.pallas_call(
        windows_kernel,
        out_shape=jax.ShapeDtypeStruct((GROUPS, LW * members, LANES), BF),
        scratch_shapes=[pltpu.VMEM(((LON + 4) * members, LANES), F32)],
        compiler_params=params(),
        cost_estimate=cost(0, 1700000),
    )(rows)


def pack_kernel(row_ref, own_ref, packed_ref):
    for row in range(ROWS):
        lanes = slice(row * C, (row + 1) * C)

        @pl.when(row_ref[0] == row)
        def _():
            packed_ref[...] = jnp.concatenate([own_ref[:PACK, :, lanes], own_ref[LW - PACK:, :, lanes]], axis=-1)


def pack(row, own):
    return pl.pallas_call(
        pack_kernel,
        in_specs=[pl.BlockSpec(memory_space=pltpu.SMEM), pl.BlockSpec(memory_space=pltpu.VMEM)],
        out_shape=jax.ShapeDtypeStruct((PACK, M, LANES), BF),
        compiler_params=params(),
        cost_estimate=cost(0, 1300000),
    )(row.reshape(1), own)


def conv_rows(x, w_ref, count):
    total = None
    for b in range(3):
        part = jnp.dot(x[b:b + count].reshape(count * M, x.shape[-1]), w_ref[b], preferred_element_type=F32)
        total = part if total is None else total + part
    return total


def head_masks(lanes):
    lane = lax.broadcasted_iota(jnp.int32, (1, lanes), 1)
    head = (lane % C) // HD
    return [(head == h).astype(BF) for h in range(HEADS)]


def score_step(qk, count):
    masks = head_masks(LANES)
    q = jnp.concatenate([qk[l, :, :C] for l in range(count)], axis=-1)
    k = jnp.concatenate([qk[l, :, C:] for l in range(count)], axis=-1)
    pairs = [k[:, i * LANES:(i + 1) * LANES] for i in range(count // 2)]
    km = jnp.concatenate([jnp.concatenate([p * mask for p in pairs], axis=-1) for mask in masks], axis=0)
    return lax.dot_general(q, km, (((1,), (1,)), ((), ())), preferred_element_type=F32)


def early_kernel(mate_ref, own_ref, w_ref, s_ref, late_ref):
    step = 8
    total = None
    for i in range(LB // step):
        start = i * step
        window = slice(start + 1, start + step + 3)
        x = jnp.concatenate([mate_ref[window], own_ref[window]], axis=-1)
        qk = conv_rows(x, w_ref, step)
        late_ref[start:start + step] = qk[:, LANES:].reshape(step, M, LANES)
        part = score_step(qk[:, :LANES].astype(BF).reshape(step, M, LANES), step)
        total = part if total is None else total + part
    s_ref[...] = total


def late_kernel(near_ref, late_ref, first_ref, w_ref, s_ref):
    step = 12
    total = first_ref[...]
    for i in range(HALF // step):
        start = i * step
        x = jnp.concatenate([near_ref[start + 1 + b:start + 1 + b + step] for b in range(3)], axis=-1)
        add = jnp.dot(x.reshape(step * M, 6 * C), w_ref[...], preferred_element_type=F32)
        halves = []
        for half in range(2):
            at = half * HALF + start
            qk = late_ref[at:at + step].reshape(step * M, LANES) + add[:, half * LANES:(half + 1) * LANES]
            halves.append(qk.astype(BF).reshape(step, M, LANES))
        total = total + score_step(jnp.concatenate(halves, axis=0), 2 * step)
    for a in range(M // 8):
        for b in range(HEADS * M // 128):
            s_ref[a * (HEADS * M // 128) + b] = total[8 * a:8 * (a + 1), 128 * b:128 * (b + 1)]


def early_scores(mate, own, w_qk):
    return pl.pallas_call(
        early_kernel,
        out_shape=(jax.ShapeDtypeStruct((M, HEADS * M), F32), jax.ShapeDtypeStruct((LB, M, LANES), F32)),
        compiler_params=params(),
        cost_estimate=cost(3_000_000_000, 3000000),
    )(mate, own, w_qk)


def late_scores(near, late, first, w_near):
    tiles = HEADS * M * M // 1024
    return pl.pallas_call(
        late_kernel,
        out_shape=jax.ShapeDtypeStruct((tiles, 8, 128), F32),
        compiler_params=params(),
        cost_estimate=cost(2_000_000_000, 3000000),
    )(near, late, first, w_near)


def values_kernel(near_ref, far_ref, own_ref, mate_ref, w_ref, keep_ref, v_out, x_ref, v_ref, sems):
    half = LW // 2
    skip = half - (LW - PACK)
    x_ref[:half, :, :LANES] = jnp.concatenate([near_ref[:half, :, :C], far_ref[:half, :, :C]], axis=-1)
    x_ref[half:, :, :LANES] = jnp.concatenate([near_ref[skip:, :, C:], far_ref[skip:, :, C:]], axis=-1)
    step = 10
    w = w_ref[...].reshape(18 * C, 4 * C)
    copies = []
    for start in range(0, LV, step):
        x = jnp.concatenate(
            [ref[start + b:start + b + step] for b in range(3) for ref in (x_ref, own_ref, mate_ref)], axis=-1
        )
        v = jnp.dot(x.reshape(step * M, 18 * C), w, preferred_element_type=F32)
        piece = slice(start, start + step)
        v_ref[piece] = (v.reshape(step, M, 4 * C) * keep_ref[piece]).astype(BF)
        copies.append(pltpu.make_async_copy(v_ref.at[piece], v_out.at[piece], sems.at[start // step]))
        copies[-1].start()
    for copy in copies:
        copy.wait()


def value_maps(near, far, own, mate, w_v, keep):
    return pl.pallas_call(
        values_kernel,
        out_shape=pltpu.HBM((LV, M, 4 * C), BF),
        out_specs=pl.BlockSpec(memory_space=pltpu.HBM),
        scratch_shapes=[
            pltpu.VMEM((LW, M, LANES), BF),
            pltpu.VMEM((LV, M, 4 * C), BF),
            pltpu.SemaphoreType.DMA((5,)),
        ],
        compiler_params=params(),
        cost_estimate=cost(2_000_000_000, 4000000),
    )(near, far, own, mate, w_v, keep)


def mix_kernel(attn_ref, v_in, own_ref, w_ref, out_ref, v_ref, att_ref, sems):
    pieces = 5
    size = LV // pieces
    copies = [
        pltpu.make_async_copy(v_in.at[i * size:(i + 1) * size], v_ref.at[i * size:(i + 1) * size], sems.at[i])
        for i in range(pieces)
    ]
    for copy in copies:
        copy.start()
    masks = head_masks(4 * C)
    lane_tiles = HEADS * M // 128
    attn = jnp.concatenate(
        [jnp.concatenate([attn_ref[a * lane_tiles + b] for b in range(lane_tiles)], axis=-1) for a in range(M // 8)],
        axis=0,
    )
    for i in range(pieces):
        copies[i].wait()
        for t in range(i * size, (i + 1) * size):
            v = v_ref[t]
            vm = jnp.concatenate([v * mask for mask in masks], axis=0)
            att_ref[t] = jnp.dot(attn, vm, preferred_element_type=F32).astype(BF)
    step = 8
    for start in range(0, LB, step):
        total = own_ref[start + 2:start + 2 + step].astype(F32).reshape(step * M, LANES)
        for b in range(3):
            x = att_ref[start + b:start + b + step].reshape(step * M, 4 * C)
            total = total + jnp.dot(x, w_ref[b], preferred_element_type=F32)
        out_ref[start:start + step] = total.astype(BF).reshape(step, M, LANES)


def mix(attn, v, own, w_o):
    vmem = pl.BlockSpec(memory_space=pltpu.VMEM)
    hbm = pl.BlockSpec(memory_space=pltpu.HBM)
    return pl.pallas_call(
        mix_kernel,
        in_specs=[vmem, hbm, vmem, vmem],
        out_shape=jax.ShapeDtypeStruct((LB, M, LANES), BF),
        scratch_shapes=[
            pltpu.VMEM((LV, M, 4 * C), BF),
            pltpu.VMEM((LV, M, 4 * C), BF),
            pltpu.SemaphoreType.DMA((5,)),
        ],
        compiler_params=params(),
        cost_estimate=cost(4_000_000_000, 4000000),
    )(attn, pltpu.with_memory_space_constraint(v, pltpu.HBM), own, w_o)


def local(fields, w_qkv, w_out):
    members_here = fields.shape[0]
    core = lax.axis_index("core")
    place = lax.axis_index(SPACE)
    group = lax.axis_index("mem")
    places = lax.axis_size(SPACE)
    last_place = places - 1
    w_qk, w_near, w_v, w_o = place_weights(core, w_qkv, w_out)

    rows = jnp.transpose(fields, (0, 2, 1, 3)).reshape(members_here, LANES, LON)
    windows = windows_of(rows).reshape(GROUPS, LW, members_here, LANES)
    arrived = lax.all_to_all(windows, "mem", split_axis=0, concat_axis=0, tiled=True)
    own = jnp.transpose(arrived, (1, 0, 2, 3)).reshape(LW, M, LANES)
    seams = [(i, i + 1) for i in range(1, last_place, 2)]
    seams = seams + [(j, i) for i, j in seams]
    mate = lax.ppermute(own, "core", [(0, 1), (1, 0)])
    near = lax.ppermute(pack(core, own), SPACE, seams)
    far = lax.ppermute(pack(1 - core, own), SPACE, seams)

    first, late = early_scores(mate, own, w_qk)
    part = late_scores(near, late, first, w_near)
    part = lax.all_to_all(part, SPACE, split_axis=0, concat_axis=0, tiled=True)
    part = part.reshape((places, -1) + part.shape[1:]).sum(axis=0)
    part = jnp.broadcast_to(part[None], (GROUPS,) + part.shape)
    part = lax.all_to_all(part, "mem", split_axis=0, concat_axis=0, tiled=True)

    row = lax.broadcasted_iota(jnp.int32, (LV, 1, 4 * C), 2) // C
    lon = lax.broadcasted_iota(jnp.int32, (LV, 1, 4 * C), 0)
    outside = (
        ((row == 0) & (place == 0))
        | ((row == 3) & (place == last_place))
        | ((lon == 0) & (group == 0))
        | ((lon == LV - 1) & (group == GROUPS - 1))
    )
    keep = jnp.where(outside, 0.0, 1.0).astype(F32)
    v = value_maps(near, far, own, mate, w_v, keep)
    part, v = lax.optimization_barrier((part, v))
    total = part.sum(axis=0)
    scale = 1.0 / math.sqrt(HD * ROWS * places * LON)
    attn = jax.nn.softmax((total * scale).reshape(total.shape[:-1] + (2, M)), axis=-1).astype(BF).reshape(total.shape)
    attn = jnp.broadcast_to(attn[None], (places,) + attn.shape).reshape(-1, 8, 128)
    attn = lax.all_to_all(attn, SPACE, split_axis=0, concat_axis=0, tiled=True)
    mixed = mix(attn, v, own, w_o)
    mixed = jnp.transpose(mixed.reshape(LB, GROUPS, members_here, LANES), (1, 0, 2, 3))
    back = lax.all_to_all(mixed, "mem", split_axis=0, concat_axis=0, tiled=True)
    back = jnp.transpose(back.reshape(LON, members_here, LANES), (1, 2, 0))
    back = lax.optimization_barrier(back).reshape(members_here, ROWS, C, LON)
    return jnp.transpose(back, (0, 2, 1, 3))


def solution(mesh):
    whole = Mesh(mesh.devices.reshape(4, 4, 2, 8), ("x", "y", "core", "mem"))
    return jax.shard_map(
        local,
        mesh=whole,
        in_specs=(P("mem", None, SPACE, None), P(), P()),
        out_specs=P("mem", None, SPACE, None),
        check_vma=False,
    )
```

```python
import functools
import math

import jax
import jax.numpy as jnp
from jax import lax
from jax.experimental import pallas as pl
from jax.experimental.pallas import tpu as pltpu
from jax.sharding import Mesh
from jax.sharding import PartitionSpec as P

C = 64
HEADS = 8
HD = 8
M = 64
ROWS = 2
LANES = ROWS * C
GROUPS = 8
LON = 384
LB = LON // GROUPS
LW = LB + 4
LV = LB + 2
HALF = LB // 2
PACK = HALF + 4
SPACE = ("x", "y", "core")
BF = jnp.bfloat16
F32 = jnp.float32
VMEM_LIMIT = 24 * 1024 * 1024


def place_weights_kernel(core_ref, w_ref, wo_ref, qk_ref, near_ref, v_ref, o_ref, plain_ref):
    for ref in (qk_ref, near_ref, plain_ref):
        ref[...] = jnp.zeros(ref.shape, BF)
    new = lax.broadcasted_iota(jnp.int32, (4 * C, 4 * C), 0)
    old = lax.broadcasted_iota(jnp.int32, (4 * C, 4 * C), 1)
    wanted = new % (4 * HD) // HD * C + new // (4 * HD) * HD + new % HD
    order = (wanted == old).astype(BF)

    def span(i):
        return slice(i * C, (i + 1) * C)

    def place(core):
        early, late = 1 - core, core
        near = -1 if core == 0 else 2
        far = -2 if core == 0 else 3
        mate = 2 if core == 0 else -2
        in_pair = {mate: 0, mate + 1: 1, 0: 2, 1: 3}
        in_all = {near: 0, far: 1, 0: 2, 1: 3, mate: 4, mate + 1: 5}
        for b in range(3):
            for a in range(3):
                tap = w_ref[3 * a + b]
                for out, part in ((early, 0), (late, 2)):
                    row = out + a - 1
                    if row in in_pair:
                        qk_ref[b, span(in_pair[row]), span(part)] = tap[:, 0:C]
                        qk_ref[b, span(in_pair[row]), span(part + 1)] = tap[:, C:2 * C]
                    else:
                        for half in range(2):
                            near_ref[span(2 * b + half), span(2 * half)] = tap[:, 0:C]
                            near_ref[span(2 * b + half), span(2 * half + 1)] = tap[:, C:2 * C]
                for out in range(-1, 3):
                    plain_ref[b, span(in_all[out + a - 1]), span(out + 1)] = tap[:, 2 * C:3 * C]

    pl.when(core_ref[0] == 0)(lambda: place(0))
    pl.when(core_ref[0] == 1)(lambda: place(1))
    for b in range(3):
        v_ref[b] = lax.dot_general(
            plain_ref[b], order, (((1,), (1,)), ((), ())), preferred_element_type=F32
        ).astype(BF)
    plain_ref[...] = jnp.zeros(plain_ref.shape, BF)
    for b in range(3):
        for a in range(3):
            for out in range(2):
                plain_ref[b, span(out + a), span(out)] = wo_ref[3 * a + b]
        o_ref[b] = jnp.dot(order, plain_ref[b, :4 * C, :2 * C], preferred_element_type=F32).astype(BF)


def params():
    return pltpu.CompilerParams(vmem_limit_bytes=VMEM_LIMIT)


def cost(flops, moved):
    return pl.CostEstimate(flops=flops, bytes_accessed=moved, transcendentals=0)


def place_weights(core, w_qkv, w_out):
    vmem = pl.BlockSpec(memory_space=pltpu.VMEM)
    return pl.pallas_call(
        place_weights_kernel,
        in_specs=[pl.BlockSpec(memory_space=pltpu.SMEM), vmem, vmem],
        out_shape=(
            jax.ShapeDtypeStruct((3, 4 * C, 4 * C), BF),
            jax.ShapeDtypeStruct((6 * C, 4 * C), BF),
            jax.ShapeDtypeStruct((3, 6 * C, 4 * C), BF),
            jax.ShapeDtypeStruct((3, 4 * C, 2 * C), BF),
        ),
        scratch_shapes=[pltpu.VMEM((3, 6 * C, 4 * C), BF)],
        compiler_params=params(),
        cost_estimate=cost(0, 1500000),
    )(core.reshape(1), jnp.swapaxes(w_qkv, 1, 2), jnp.swapaxes(w_out, 1, 2))


def windows_kernel(rows_ref, out_ref, cells_ref):
    members = rows_ref.shape[0]
    edge = 2 * members
    cells_ref[:edge] = jnp.zeros((edge, LANES), F32)
    cells_ref[edge + LON * members:] = jnp.zeros((edge, LANES), F32)
    for m in range(members):
        cells_ref[pl.ds(edge + m, LON, stride=members)] = rows_ref[m].astype(F32).T
    for g in range(GROUPS):
        start = g * LB * members
        out_ref[g] = cells_ref[start:start + LW * members].astype(BF)


def windows_of(rows):
    members = rows.shape[0]
    return pl.pallas_call(
        windows_kernel,
        out_shape=jax.ShapeDtypeStruct((GROUPS, LW * members, LANES), BF),
        scratch_shapes=[pltpu.VMEM(((LON + 4) * members, LANES), F32)],
        compiler_params=params(),
        cost_estimate=cost(0, 1700000),
    )(rows)


def pack_kernel(row_ref, own_ref, packed_ref):
    for row in range(ROWS):
        lanes = slice(row * C, (row + 1) * C)

        @pl.when(row_ref[0] == row)
        def _():
            packed_ref[...] = jnp.concatenate([own_ref[:PACK, :, lanes], own_ref[LW - PACK:, :, lanes]], axis=-1)


def pack(row, own):
    return pl.pallas_call(
        pack_kernel,
        in_specs=[pl.BlockSpec(memory_space=pltpu.SMEM), pl.BlockSpec(memory_space=pltpu.VMEM)],
        out_shape=jax.ShapeDtypeStruct((PACK, M, LANES), BF),
        compiler_params=params(),
        cost_estimate=cost(0, 1300000),
    )(row.reshape(1), own)


def conv_rows(x, w_ref, count):
    total = None
    for b in range(3):
        part = jnp.dot(x[b:b + count].reshape(count * M, x.shape[-1]), w_ref[b], preferred_element_type=F32)
        total = part if total is None else total + part
    return total


def head_masks(lanes):
    lane = lax.broadcasted_iota(jnp.int32, (1, lanes), 1)
    head = (lane % C) // HD
    return [(head == h).astype(BF) for h in range(HEADS)]


def score_step(qk, count):
    masks = head_masks(LANES)
    q = jnp.concatenate([qk[l, :, :C] for l in range(count)], axis=-1)
    k = jnp.concatenate([qk[l, :, C:] for l in range(count)], axis=-1)
    pairs = [k[:, i * LANES:(i + 1) * LANES] for i in range(count // 2)]
    km = jnp.concatenate([jnp.concatenate([p * mask for p in pairs], axis=-1) for mask in masks], axis=0)
    return lax.dot_general(q, km, (((1,), (1,)), ((), ())), preferred_element_type=F32)


def early_kernel(mate_ref, own_ref, w_ref, s_ref, late_ref):
    step = 8
    total = None
    for i in range(LB // step):
        start = i * step
        window = slice(start + 1, start + step + 3)
        x = jnp.concatenate([mate_ref[window], own_ref[window]], axis=-1)
        qk = conv_rows(x, w_ref, step)
        late_ref[start:start + step] = qk[:, LANES:].reshape(step, M, LANES)
        part = score_step(qk[:, :LANES].astype(BF).reshape(step, M, LANES), step)
        total = part if total is None else total + part
    s_ref[...] = total


def late_kernel(near_ref, late_ref, first_ref, w_ref, s_ref):
    step = 12
    total = first_ref[...]
    for i in range(HALF // step):
        start = i * step
        x = jnp.concatenate([near_ref[start + 1 + b:start + 1 + b + step] for b in range(3)], axis=-1)
        add = jnp.dot(x.reshape(step * M, 6 * C), w_ref[...], preferred_element_type=F32)
        halves = []
        for half in range(2):
            at = half * HALF + start
            qk = late_ref[at:at + step].reshape(step * M, LANES) + add[:, half * LANES:(half + 1) * LANES]
            halves.append(qk.astype(BF).reshape(step, M, LANES))
        total = total + score_step(jnp.concatenate(halves, axis=0), 2 * step)
    for a in range(M // 8):
        for b in range(HEADS * M // 128):
            s_ref[a * (HEADS * M // 128) + b] = total[8 * a:8 * (a + 1), 128 * b:128 * (b + 1)]


def early_scores(mate, own, w_qk):
    return pl.pallas_call(
        early_kernel,
        out_shape=(jax.ShapeDtypeStruct((M, HEADS * M), F32), jax.ShapeDtypeStruct((LB, M, LANES), F32)),
        compiler_params=params(),
        cost_estimate=cost(3_000_000_000, 3000000),
    )(mate, own, w_qk)


def late_scores(near, late, first, w_near):
    tiles = HEADS * M * M // 1024
    return pl.pallas_call(
        late_kernel,
        out_shape=jax.ShapeDtypeStruct((tiles, 8, 128), F32),
        compiler_params=params(),
        cost_estimate=cost(2_000_000_000, 3000000),
    )(near, late, first, w_near)


def values_kernel(near_ref, far_ref, own_ref, mate_ref, w_ref, keep_ref, v_out, x_ref, v_ref, sems):
    half = LW // 2
    skip = half - (LW - PACK)
    x_ref[:half, :, :LANES] = jnp.concatenate([near_ref[:half, :, :C], far_ref[:half, :, :C]], axis=-1)
    x_ref[half:, :, :LANES] = jnp.concatenate([near_ref[skip:, :, C:], far_ref[skip:, :, C:]], axis=-1)
    step = 10
    w = w_ref[...].reshape(18 * C, 4 * C)
    copies = []
    for start in range(0, LV, step):
        x = jnp.concatenate(
            [ref[start + b:start + b + step] for b in range(3) for ref in (x_ref, own_ref, mate_ref)], axis=-1
        )
        v = jnp.dot(x.reshape(step * M, 18 * C), w, preferred_element_type=F32)
        piece = slice(start, start + step)
        v_ref[piece] = (v.reshape(step, M, 4 * C) * keep_ref[piece]).astype(BF)
        copies.append(pltpu.make_async_copy(v_ref.at[piece], v_out.at[piece], sems.at[start // step]))
        copies[-1].start()
    for copy in copies:
        copy.wait()


def value_maps(near, far, own, mate, w_v, keep):
    return pl.pallas_call(
        values_kernel,
        out_shape=pltpu.HBM((LV, M, 4 * C), BF),
        out_specs=pl.BlockSpec(memory_space=pltpu.HBM),
        scratch_shapes=[
            pltpu.VMEM((LW, M, LANES), BF),
            pltpu.VMEM((LV, M, 4 * C), BF),
            pltpu.SemaphoreType.DMA((5,)),
        ],
        compiler_params=params(),
        cost_estimate=cost(2_000_000_000, 4000000),
    )(near, far, own, mate, w_v, keep)


def mix_kernel(attn_ref, v_in, own_ref, w_ref, out_ref, v_ref, att_ref, sems):
    pieces = 5
    size = LV // pieces
    copies = [
        pltpu.make_async_copy(v_in.at[i * size:(i + 1) * size], v_ref.at[i * size:(i + 1) * size], sems.at[i])
        for i in range(pieces)
    ]
    for copy in copies:
        copy.start()
    lane = lax.broadcasted_iota(jnp.int32, (1, 4 * C), 1) % LANES
    masks = [(lane // (4 * HD) == h).astype(BF) for h in range(HEADS // 2)]
    lane_tiles = HEADS * M // 128
    attn = jnp.concatenate(
        [jnp.concatenate([attn_ref[a * lane_tiles + b] for b in range(lane_tiles)], axis=-1) for a in range(M // 8)],
        axis=0,
    )
    for i in range(pieces):
        copies[i].wait()
        for t in range(i * size, (i + 1) * size, 2):
            for half in range(2):
                lanes = slice(half * LANES, (half + 1) * LANES)
                v = jnp.concatenate([v_ref[t, :, lanes], v_ref[t + 1, :, lanes]], axis=-1)
                vm = jnp.concatenate([v * mask for mask in masks], axis=0)
                weights = attn[:, half * 4 * M:(half + 1) * 4 * M]
                blended = jnp.dot(weights, vm, preferred_element_type=F32).astype(BF)
                att_ref[t, :, lanes] = blended[:, :LANES]
                att_ref[t + 1, :, lanes] = blended[:, LANES:]
    step = 8
    for start in range(0, LB, step):
        total = own_ref[start + 2:start + 2 + step].astype(F32).reshape(step * M, LANES)
        for b in range(3):
            x = att_ref[start + b:start + b + step].reshape(step * M, 4 * C)
            total = total + jnp.dot(x, w_ref[b], preferred_element_type=F32)
        out_ref[start:start + step] = total.astype(BF).reshape(step, M, LANES)


def mix(attn, v, own, w_o):
    vmem = pl.BlockSpec(memory_space=pltpu.VMEM)
    hbm = pl.BlockSpec(memory_space=pltpu.HBM)
    return pl.pallas_call(
        mix_kernel,
        in_specs=[vmem, hbm, vmem, vmem],
        out_shape=jax.ShapeDtypeStruct((LB, M, LANES), BF),
        scratch_shapes=[
            pltpu.VMEM((LV, M, 4 * C), BF),
            pltpu.VMEM((LV, M, 4 * C), BF),
            pltpu.SemaphoreType.DMA((5,)),
        ],
        compiler_params=params(),
        cost_estimate=cost(4_000_000_000, 4000000),
    )(attn, pltpu.with_memory_space_constraint(v, pltpu.HBM), own, w_o)


def total_kernel(parts_ref, out_ref):
    total = parts_ref[0]
    for i in range(1, parts_ref.shape[0]):
        total = total + parts_ref[i]
    for g in range(out_ref.shape[0]):
        out_ref[g] = total


def summed(parts, copies):
    return pl.pallas_call(
        total_kernel,
        out_shape=jax.ShapeDtypeStruct((copies,) + parts.shape[1:], F32),
        compiler_params=params(),
        cost_estimate=cost(0, 300000),
    )(parts)


def softmax_kernel(scale, parts_ref, out_ref):
    total = parts_ref[0]
    for i in range(1, parts_ref.shape[0]):
        total = total + parts_ref[i]
    total = total * scale
    low = lax.broadcasted_iota(jnp.int32, total.shape, 1) < M

    def halves(reduce, x, fill):
        first = reduce(jnp.where(low, x, fill), axis=-1, keepdims=True)
        second = reduce(jnp.where(low, fill, x), axis=-1, keepdims=True)
        return jnp.where(low, first, second)

    e = jnp.exp(total - halves(jnp.max, total, -jnp.inf))
    attn = (e / halves(jnp.sum, e, 0.0)).astype(BF)
    for g in range(out_ref.shape[0]):
        out_ref[g] = attn


def softmax_of(parts, scale, copies):
    return pl.pallas_call(
        functools.partial(softmax_kernel, scale),
        out_shape=jax.ShapeDtypeStruct((copies,) + parts.shape[1:], BF),
        compiler_params=params(),
        cost_estimate=cost(0, 300000),
    )(parts)


def final_kernel(back_ref, out_ref, cells_ref):
    members = out_ref.shape[0]
    count = LB * members
    for g in range(GROUPS):
        cells_ref[g * count:(g + 1) * count] = back_ref[g].astype(F32)
    for m in range(members):
        rows = cells_ref[pl.ds(m, LON, stride=members)].T
        for r in range(ROWS):
            out_ref[m, :, r] = rows[r * C:(r + 1) * C].astype(BF)


def final_layout(back):
    members = back.shape[1] // LB
    return pl.pallas_call(
        final_kernel,
        out_shape=jax.ShapeDtypeStruct((members, C, ROWS, LON), BF),
        scratch_shapes=[pltpu.VMEM((LON * members, LANES), F32)],
        compiler_params=params(),
        cost_estimate=cost(0, 1600000),
    )(back)


def local(fields, w_qkv, w_out):
    members_here = fields.shape[0]
    core = lax.axis_index("core")
    place = lax.axis_index(SPACE)
    group = lax.axis_index("mem")
    places = lax.axis_size(SPACE)
    last_place = places - 1

    rows = jnp.transpose(fields, (0, 2, 1, 3)).reshape(members_here, LANES, LON)
    windows = windows_of(rows).reshape(GROUPS, LW, members_here, LANES)
    arrived = lax.all_to_all(windows, "mem", split_axis=0, concat_axis=0, tiled=True)
    own = jnp.transpose(arrived, (1, 0, 2, 3)).reshape(LW, M, LANES)
    seams = [(i, i + 1) for i in range(1, last_place, 2)]
    seams = seams + [(j, i) for i, j in seams]
    near = lax.ppermute(pack(core, own), SPACE, seams)
    mate = lax.ppermute(own, "core", [(0, 1), (1, 0)])
    far = lax.ppermute(pack(1 - core, own), SPACE, seams)
    w_qk, w_near, w_v, w_o = place_weights(core, w_qkv, w_out)
    first, late = early_scores(mate, own, w_qk)
    part = late_scores(near, late, first, w_near)

    row = lax.broadcasted_iota(jnp.int32, (LV, 1, 4 * C), 2) % (4 * HD) // HD
    lon = lax.broadcasted_iota(jnp.int32, (LV, 1, 4 * C), 0)
    outside = (
        ((row == 0) & (place == 0))
        | ((row == 3) & (place == last_place))
        | ((lon == 0) & (group == 0))
        | ((lon == LV - 1) & (group == GROUPS - 1))
    )
    keep = jnp.where(outside, 0.0, 1.0).astype(F32)
    part = lax.all_to_all(part, SPACE, split_axis=0, concat_axis=0, tiled=True)
    v = value_maps(near, far, own, mate, w_v, keep)
    part, v = lax.optimization_barrier((part, v))
    part = lax.all_to_all(summed(part, GROUPS), "mem", split_axis=0, concat_axis=0, tiled=True)
    attn = softmax_of(part, 1.0 / math.sqrt(HD * ROWS * places * LON), places)
    attn = lax.all_to_all(attn, SPACE, split_axis=0, concat_axis=0, tiled=True)
    mixed = mix(attn, v, own, w_o)
    mixed = jnp.transpose(mixed.reshape(LB, GROUPS, members_here, LANES), (1, 0, 2, 3))
    back = lax.all_to_all(mixed, "mem", split_axis=0, concat_axis=0, tiled=True)
    return final_layout(back.reshape(GROUPS, LB * members_here, LANES))


def solution(mesh):
    whole = Mesh(mesh.devices.reshape(4, 4, 2, 8), ("x", "y", "core", "mem"))
    return jax.shard_map(
        local,
        mesh=whole,
        in_specs=(P("mem", None, SPACE, None), P(), P()),
        out_specs=P("mem", None, SPACE, None),
        check_vma=False,
    )
```

```python
import functools
import math

import jax
import jax.numpy as jnp
from jax import lax
from jax.experimental import pallas as pl
from jax.experimental.pallas import tpu as pltpu
from jax.sharding import Mesh
from jax.sharding import PartitionSpec as P

C = 64
HEADS = 8
HD = 8
M = 64
ROWS = 2
LANES = ROWS * C
GROUPS = 8
LON = 384
LB = LON // GROUPS
LW = LB + 4
LV = LB + 2
HALF = LB // 2
PACK = HALF + 4
SPACE = ("x", "y", "core")
BF = jnp.bfloat16
F32 = jnp.float32
VMEM_LIMIT = 24 * 1024 * 1024


def place_weights_kernel(core_ref, w_ref, wo_ref, qk_ref, near_ref, v_ref, o_ref, plain_ref):
    for ref in (qk_ref, near_ref, plain_ref):
        ref[...] = jnp.zeros(ref.shape, BF)
    new = lax.broadcasted_iota(jnp.int32, (4 * C, 4 * C), 0)
    old = lax.broadcasted_iota(jnp.int32, (4 * C, 4 * C), 1)
    wanted = new % (4 * HD) // HD * C + new // (4 * HD) * HD + new % HD
    order = (wanted == old).astype(BF)

    def span(i):
        return slice(i * C, (i + 1) * C)

    def place(core):
        early, late = 1 - core, core
        near = -1 if core == 0 else 2
        far = -2 if core == 0 else 3
        mate = 2 if core == 0 else -2
        in_pair = {mate: 0, mate + 1: 1, 0: 2, 1: 3}
        in_all = {near: 0, far: 1, 0: 2, 1: 3, mate: 4, mate + 1: 5}
        for b in range(3):
            for a in range(3):
                tap = w_ref[3 * a + b]
                for out, part in ((early, 0), (late, 2)):
                    row = out + a - 1
                    if row in in_pair:
                        qk_ref[b, span(in_pair[row]), span(part)] = tap[:, 0:C]
                        qk_ref[b, span(in_pair[row]), span(part + 1)] = tap[:, C:2 * C]
                    else:
                        for half in range(2):
                            near_ref[span(2 * b + half), span(2 * half)] = tap[:, 0:C]
                            near_ref[span(2 * b + half), span(2 * half + 1)] = tap[:, C:2 * C]
                for out in range(-1, 3):
                    plain_ref[b, span(in_all[out + a - 1]), span(out + 1)] = tap[:, 2 * C:3 * C]

    pl.when(core_ref[0] == 0)(lambda: place(0))
    pl.when(core_ref[0] == 1)(lambda: place(1))
    for b in range(3):
        v_ref[b] = lax.dot_general(
            plain_ref[b], order, (((1,), (1,)), ((), ())), preferred_element_type=F32
        ).astype(BF)
    plain_ref[...] = jnp.zeros(plain_ref.shape, BF)
    for b in range(3):
        for a in range(3):
            for out in range(2):
                plain_ref[b, span(out + a), span(out)] = wo_ref[3 * a + b]
        o_ref[b] = jnp.dot(order, plain_ref[b, :4 * C, :2 * C], preferred_element_type=F32).astype(BF)


def params():
    return pltpu.CompilerParams(vmem_limit_bytes=VMEM_LIMIT)


def cost(flops, moved):
    return pl.CostEstimate(flops=flops, bytes_accessed=moved, transcendentals=0)


def place_weights(core, w_qkv, w_out):
    vmem = pl.BlockSpec(memory_space=pltpu.VMEM)
    return pl.pallas_call(
        place_weights_kernel,
        in_specs=[pl.BlockSpec(memory_space=pltpu.SMEM), vmem, vmem],
        out_shape=(
            jax.ShapeDtypeStruct((3, 4 * C, 4 * C), BF),
            jax.ShapeDtypeStruct((6 * C, 4 * C), BF),
            jax.ShapeDtypeStruct((3, 6 * C, 4 * C), BF),
            jax.ShapeDtypeStruct((3, 4 * C, 2 * C), BF),
        ),
        scratch_shapes=[pltpu.VMEM((3, 6 * C, 4 * C), BF)],
        compiler_params=params(),
        cost_estimate=cost(0, 1500000),
    )(core.reshape(1), jnp.swapaxes(w_qkv, 1, 2), jnp.swapaxes(w_out, 1, 2))


def windows_kernel(rows_ref, out_ref, cells_ref):
    members = rows_ref.shape[0]
    edge = 2 * members
    cells_ref[:edge] = jnp.zeros((edge, LANES), F32)
    cells_ref[edge + LON * members:] = jnp.zeros((edge, LANES), F32)
    for m in range(members):
        cells_ref[pl.ds(edge + m, LON, stride=members)] = rows_ref[m].astype(F32).T
    for g in range(GROUPS):
        start = g * LB * members
        out_ref[g] = cells_ref[start:start + LW * members].astype(BF)


def windows_of(rows):
    members = rows.shape[0]
    return pl.pallas_call(
        windows_kernel,
        out_shape=jax.ShapeDtypeStruct((GROUPS, LW * members, LANES), BF),
        scratch_shapes=[pltpu.VMEM(((LON + 4) * members, LANES), F32)],
        compiler_params=params(),
        cost_estimate=cost(0, 1700000),
    )(rows)


def pack_kernel(row_ref, own_ref, packed_ref):
    for row in range(ROWS):
        lanes = slice(row * C, (row + 1) * C)

        @pl.when(row_ref[0] == row)
        def _():
            packed_ref[...] = jnp.concatenate([own_ref[:PACK, :, lanes], own_ref[LW - PACK:, :, lanes]], axis=-1)


def pack(row, own):
    return pl.pallas_call(
        pack_kernel,
        in_specs=[pl.BlockSpec(memory_space=pltpu.SMEM), pl.BlockSpec(memory_space=pltpu.VMEM)],
        out_shape=jax.ShapeDtypeStruct((PACK, M, LANES), BF),
        compiler_params=params(),
        cost_estimate=cost(0, 1300000),
    )(row.reshape(1), own)


def conv_rows(x, w_ref, count):
    total = None
    for b in range(3):
        part = jnp.dot(x[b:b + count].reshape(count * M, x.shape[-1]), w_ref[b], preferred_element_type=F32)
        total = part if total is None else total + part
    return total


def head_masks(lanes):
    lane = lax.broadcasted_iota(jnp.int32, (1, lanes), 1)
    head = (lane % C) // HD
    return [(head == h).astype(BF) for h in range(HEADS)]


def score_step(qk, count):
    masks = head_masks(LANES)
    q = jnp.concatenate([qk[l, :, :C] for l in range(count)], axis=-1)
    k = jnp.concatenate([qk[l, :, C:] for l in range(count)], axis=-1)
    pairs = [k[:, i * LANES:(i + 1) * LANES] for i in range(count // 2)]
    km = jnp.concatenate([jnp.concatenate([p * mask for p in pairs], axis=-1) for mask in masks], axis=0)
    return lax.dot_general(q, km, (((1,), (1,)), ((), ())), preferred_element_type=F32)


def score_step_by_half(qk, count):
    lane = lax.broadcasted_iota(jnp.int32, (1, LANES), 1)
    masks = [(lane % (C // 2) // HD == h).astype(BF) for h in range(HEADS // 2)]
    parts = []
    for start in (0, C // 2):
        q = jnp.concatenate([qk[l, :, start:start + C // 2] for l in range(count)], axis=-1)
        k = jnp.concatenate([qk[l, :, C + start:C + start + C // 2] for l in range(count)], axis=-1)
        tiles = [k[:, i * LANES:(i + 1) * LANES] for i in range(count // 4)]
        km = jnp.concatenate([jnp.concatenate([t * mask for t in tiles], axis=-1) for mask in masks], axis=0)
        parts.append(lax.dot_general(q, km, (((1,), (1,)), ((), ())), preferred_element_type=F32))
    return jnp.concatenate(parts, axis=-1)


def early_kernel(mate_ref, own_ref, w_ref, s_ref, late_ref):
    step, joined = 8, 3
    total = None
    held = []
    for start in range(0, LB, step):
        window = slice(start + 1, start + step + 3)
        x = jnp.concatenate([mate_ref[window], own_ref[window]], axis=-1)
        qk = conv_rows(x, w_ref, step)
        late_ref[start:start + step] = qk[:, LANES:].reshape(step, M, LANES)
        held.append(qk[:, :LANES].astype(BF).reshape(step, M, LANES))
        if len(held) == joined:
            part = score_step(jnp.concatenate(held, axis=0), step * joined)
            total = part if total is None else total + part
            held = []
    s_ref[...] = total


def late_kernel(near_ref, late_ref, first_ref, w_ref, s_ref, near_out, sems):
    copy = pltpu.make_async_copy(near_ref, near_out, sems.at[0])
    copy.start()
    step = 6
    total = first_ref[...]
    for start in range(0, HALF, step):
        x = jnp.concatenate([near_ref[start + 1 + b:start + 1 + b + step] for b in range(3)], axis=-1)
        add = jnp.dot(x.reshape(step * M, 6 * C), w_ref[...], preferred_element_type=F32)
        halves = []
        for half in range(2):
            at = half * HALF + start
            qk = late_ref[at:at + step].reshape(step * M, LANES) + add[:, half * LANES:(half + 1) * LANES]
            halves.append(qk.astype(BF).reshape(step, M, LANES))
        total = total + score_step_by_half(jnp.concatenate(halves, axis=0), 2 * step)
    for a in range(M // 8):
        for b in range(HEADS * M // 128):
            s_ref[a * (HEADS * M // 128) + b] = total[8 * a:8 * (a + 1), 128 * b:128 * (b + 1)]
    copy.wait()


def early_scores(mate, own, w_qk):
    return pl.pallas_call(
        early_kernel,
        out_shape=(jax.ShapeDtypeStruct((M, HEADS * M), F32), jax.ShapeDtypeStruct((LB, M, LANES), F32)),
        compiler_params=params(),
        cost_estimate=cost(3_000_000_000, 3000000),
    )(mate, own, w_qk)


def late_scores(near, late, first, w_near):
    tiles = HEADS * M * M // 1024
    return pl.pallas_call(
        late_kernel,
        out_shape=(jax.ShapeDtypeStruct((tiles, 8, 128), F32), pltpu.HBM(near.shape, BF)),
        out_specs=(pl.BlockSpec(memory_space=pltpu.VMEM), pl.BlockSpec(memory_space=pltpu.HBM)),
        scratch_shapes=[pltpu.SemaphoreType.DMA((1,))],
        compiler_params=params(),
        cost_estimate=cost(2_000_000_000, 3000000),
    )(near, late, first, w_near)


def values_kernel(near_in, far_in, own_ref, mate_ref, w_ref, keep_ref, v_out, near_ref, far_ref, x_ref, v_ref, sems):
    arriving = [
        pltpu.make_async_copy(near_in, near_ref, sems.at[5]),
        pltpu.make_async_copy(far_in, far_ref, sems.at[6]),
    ]
    for copy in arriving:
        copy.start()
    for copy in arriving:
        copy.wait()
    half = LW // 2
    skip = half - (LW - PACK)
    x_ref[:half, :, :LANES] = jnp.concatenate([near_ref[:half, :, :C], far_ref[:half, :, :C]], axis=-1)
    x_ref[half:, :, :LANES] = jnp.concatenate([near_ref[skip:, :, C:], far_ref[skip:, :, C:]], axis=-1)
    step = 10
    w = w_ref[...].reshape(18 * C, 4 * C)
    copies = []
    for start in range(0, LV, step):
        x = jnp.concatenate(
            [ref[start + b:start + b + step] for b in range(3) for ref in (x_ref, own_ref, mate_ref)], axis=-1
        )
        v = jnp.dot(x.reshape(step * M, 18 * C), w, preferred_element_type=F32)
        piece = slice(start, start + step)
        v_ref[piece] = (v.reshape(step, M, 4 * C) * keep_ref[piece]).astype(BF)
        copies.append(pltpu.make_async_copy(v_ref.at[piece], v_out.at[piece], sems.at[start // step]))
        copies[-1].start()
    for copy in copies:
        copy.wait()


def value_maps(near, far, own, mate, w_v, keep):
    vmem = pl.BlockSpec(memory_space=pltpu.VMEM)
    hbm = pl.BlockSpec(memory_space=pltpu.HBM)
    return pl.pallas_call(
        values_kernel,
        in_specs=[hbm, hbm, vmem, vmem, vmem, vmem],
        out_shape=pltpu.HBM((LV, M, 4 * C), BF),
        out_specs=hbm,
        scratch_shapes=[
            pltpu.VMEM((PACK, M, LANES), BF),
            pltpu.VMEM((PACK, M, LANES), BF),
            pltpu.VMEM((LW, M, LANES), BF),
            pltpu.VMEM((LV, M, 4 * C), BF),
            pltpu.SemaphoreType.DMA((7,)),
        ],
        compiler_params=params(),
        cost_estimate=cost(2_000_000_000, 4000000),
    )(pltpu.with_memory_space_constraint(near, pltpu.HBM), pltpu.with_memory_space_constraint(far, pltpu.HBM), own, mate, w_v, keep)


def mix_kernel(attn_ref, v_in, own_ref, w_ref, out_ref, v_ref, att_ref, sems):
    pieces = (slice(0, 10), slice(10, LV))
    copies = [pltpu.make_async_copy(v_in.at[p], v_ref.at[p], sems.at[i]) for i, p in enumerate(pieces)]
    for copy in copies:
        copy.start()
    lane = lax.broadcasted_iota(jnp.int32, (1, 4 * C), 1) % LANES
    masks = [(lane // (4 * HD) == h).astype(BF) for h in range(HEADS // 2)]
    lane_tiles = HEADS * M // 128
    attn = jnp.concatenate(
        [jnp.concatenate([attn_ref[a * lane_tiles + b] for b in range(lane_tiles)], axis=-1) for a in range(M // 8)],
        axis=0,
    )
    for piece, copy in zip(pieces, copies, strict=True):
        copy.wait()
        for t in range(piece.start, piece.stop, 2):
            for half in range(2):
                lanes = slice(half * LANES, (half + 1) * LANES)
                v = jnp.concatenate([v_ref[t, :, lanes], v_ref[t + 1, :, lanes]], axis=-1)
                vm = jnp.concatenate([v * mask for mask in masks], axis=0)
                weights = attn[:, half * 4 * M:(half + 1) * 4 * M]
                blended = jnp.dot(weights, vm, preferred_element_type=F32).astype(BF)
                att_ref[t, :, lanes] = blended[:, :LANES]
                att_ref[t + 1, :, lanes] = blended[:, LANES:]
    step = 8
    for start in range(0, LB, step):
        total = own_ref[start + 2:start + 2 + step].astype(F32).reshape(step * M, LANES)
        for b in range(3):
            x = att_ref[start + b:start + b + step].reshape(step * M, 4 * C)
            total = total + jnp.dot(x, w_ref[b], preferred_element_type=F32)
        out_ref[start:start + step] = total.astype(BF).reshape(step, M, LANES)


def mix(attn, v, own, w_o):
    vmem = pl.BlockSpec(memory_space=pltpu.VMEM)
    hbm = pl.BlockSpec(memory_space=pltpu.HBM)
    return pl.pallas_call(
        mix_kernel,
        in_specs=[vmem, hbm, vmem, vmem],
        out_shape=jax.ShapeDtypeStruct((LB, M, LANES), BF),
        scratch_shapes=[
            pltpu.VMEM((LV, M, 4 * C), BF),
            pltpu.VMEM((LV, M, 4 * C), BF),
            pltpu.SemaphoreType.DMA((2,)),
        ],
        compiler_params=params(),
        cost_estimate=cost(4_000_000_000, 4000000),
    )(attn, pltpu.with_memory_space_constraint(v, pltpu.HBM), own, w_o)


def total_kernel(parts_ref, out_ref):
    total = parts_ref[0]
    for i in range(1, parts_ref.shape[0]):
        total = total + parts_ref[i]
    for g in range(out_ref.shape[0]):
        out_ref[g] = total


def summed(parts, copies):
    return pl.pallas_call(
        total_kernel,
        out_shape=jax.ShapeDtypeStruct((copies,) + parts.shape[1:], F32),
        compiler_params=params(),
        cost_estimate=cost(0, 300000),
    )(parts)


def softmax_kernel(scale, parts_ref, out_ref):
    total = parts_ref[0]
    for i in range(1, parts_ref.shape[0]):
        total = total + parts_ref[i]
    total = total * scale
    low = lax.broadcasted_iota(jnp.int32, total.shape, 1) < M

    def halves(reduce, x, fill):
        first = reduce(jnp.where(low, x, fill), axis=-1, keepdims=True)
        second = reduce(jnp.where(low, fill, x), axis=-1, keepdims=True)
        return jnp.where(low, first, second)

    e = jnp.exp(total - halves(jnp.max, total, -jnp.inf))
    attn = (e / halves(jnp.sum, e, 0.0)).astype(BF)
    for g in range(out_ref.shape[0]):
        out_ref[g] = attn


def softmax_of(parts, scale, copies):
    return pl.pallas_call(
        functools.partial(softmax_kernel, scale),
        out_shape=jax.ShapeDtypeStruct((copies,) + parts.shape[1:], BF),
        compiler_params=params(),
        cost_estimate=cost(0, 300000),
    )(parts)


def final_kernel(back_ref, out_ref, cells_ref):
    members = out_ref.shape[0]
    count = LB * members
    for g in range(GROUPS):
        cells_ref[g * count:(g + 1) * count] = back_ref[g].astype(F32)
    for m in range(members):
        rows = cells_ref[pl.ds(m, LON, stride=members)].T
        for r in range(ROWS):
            out_ref[m, :, r] = rows[r * C:(r + 1) * C].astype(BF)


def final_layout(back):
    members = back.shape[1] // LB
    return pl.pallas_call(
        final_kernel,
        out_shape=jax.ShapeDtypeStruct((members, C, ROWS, LON), BF),
        scratch_shapes=[pltpu.VMEM((LON * members, LANES), F32)],
        compiler_params=params(),
        cost_estimate=cost(0, 1600000),
    )(back)


def local(fields, w_qkv, w_out):
    members_here = fields.shape[0]
    core = lax.axis_index("core")
    place = lax.axis_index(SPACE)
    group = lax.axis_index("mem")
    places = lax.axis_size(SPACE)
    last_place = places - 1

    rows = jnp.transpose(fields, (0, 2, 1, 3)).reshape(members_here, LANES, LON)
    windows = windows_of(rows).reshape(GROUPS, LW, members_here, LANES)
    arrived = lax.all_to_all(windows, "mem", split_axis=0, concat_axis=0, tiled=True)
    own = jnp.transpose(arrived, (1, 0, 2, 3)).reshape(LW, M, LANES)
    seams = [(i, i + 1) for i in range(1, last_place, 2)]
    seams = seams + [(j, i) for i, j in seams]
    near = lax.ppermute(pack(core, own), SPACE, seams)
    mate = lax.ppermute(own, "core", [(0, 1), (1, 0)])
    far = lax.ppermute(pack(1 - core, own), SPACE, seams)
    own, w_qkv = lax.optimization_barrier((own, w_qkv))
    w_qk, w_near, w_v, w_o = place_weights(core, w_qkv, w_out)
    first, late = early_scores(mate, own, w_qk)
    part, near = late_scores(near, late, first, w_near)

    row = lax.broadcasted_iota(jnp.int32, (LV, 1, 4 * C), 2) % (4 * HD) // HD
    lon = lax.broadcasted_iota(jnp.int32, (LV, 1, 4 * C), 0)
    outside = (
        ((row == 0) & (place == 0))
        | ((row == 3) & (place == last_place))
        | ((lon == 0) & (group == 0))
        | ((lon == LV - 1) & (group == GROUPS - 1))
    )
    keep = jnp.where(outside, 0.0, 1.0).astype(F32)
    part = lax.all_to_all(part, SPACE, split_axis=0, concat_axis=0, tiled=True)
    v = value_maps(near, far, own, mate, w_v, keep)
    part, v = lax.optimization_barrier((part, v))
    part = lax.all_to_all(summed(part, GROUPS), "mem", split_axis=0, concat_axis=0, tiled=True)
    attn = softmax_of(part, 1.0 / math.sqrt(HD * ROWS * places * LON), places)
    attn = lax.all_to_all(attn, SPACE, split_axis=0, concat_axis=0, tiled=True)
    mixed = mix(attn, v, own, w_o)
    mixed = jnp.transpose(mixed.reshape(LB, GROUPS, members_here, LANES), (1, 0, 2, 3))
    back = lax.all_to_all(mixed, "mem", split_axis=0, concat_axis=0, tiled=True)
    return final_layout(back.reshape(GROUPS, LB * members_here, LANES))


def solution(mesh):
    whole = Mesh(mesh.devices.reshape(4, 4, 2, 8), ("x", "y", "core", "mem"))
    return jax.shard_map(
        local,
        mesh=whole,
        in_specs=(P("mem", None, SPACE, None), P(), P()),
        out_specs=P("mem", None, SPACE, None),
        check_vma=False,
    )
```

```python
import functools
import math

import jax
import jax.numpy as jnp
from jax import lax
from jax.experimental import pallas as pl
from jax.experimental.pallas import tpu as pltpu
from jax.sharding import Mesh
from jax.sharding import PartitionSpec as P

C = 64
HEADS = 8
HD = 8
M = 64
ROWS = 2
LANES = ROWS * C
GROUPS = 8
LON = 384
LB = LON // GROUPS
LW = LB + 4
LV = LB + 2
HALF = LB // 2
PACK = HALF + 4
HELD = 20
SPACE = ("x", "y", "core")
BF = jnp.bfloat16
F32 = jnp.float32
VMEM_LIMIT = 24 * 1024 * 1024


def place_weights_kernel(core_ref, w_ref, wo_ref, qk_ref, near_ref, v_ref, o_ref, plain_ref):
    for ref in (qk_ref, near_ref, plain_ref):
        ref[...] = jnp.zeros(ref.shape, BF)
    new = lax.broadcasted_iota(jnp.int32, (4 * C, 4 * C), 0)
    old = lax.broadcasted_iota(jnp.int32, (4 * C, 4 * C), 1)
    wanted = new % (4 * HD) // HD * C + new // (4 * HD) * HD + new % HD
    order = (wanted == old).astype(BF)

    def span(i):
        return slice(i * C, (i + 1) * C)

    def place(core):
        early, late = 1 - core, core
        near = -1 if core == 0 else 2
        far = -2 if core == 0 else 3
        mate = 2 if core == 0 else -2
        in_pair = {mate: 0, mate + 1: 1, 0: 2, 1: 3}
        in_all = {near: 0, far: 1, 0: 2, 1: 3, mate: 4, mate + 1: 5}
        for b in range(3):
            for a in range(3):
                tap = w_ref[3 * a + b]
                for out, part in ((early, 0), (late, 2)):
                    row = out + a - 1
                    if row in in_pair:
                        qk_ref[b, span(in_pair[row]), span(part)] = tap[:, 0:C]
                        qk_ref[b, span(in_pair[row]), span(part + 1)] = tap[:, C:2 * C]
                    else:
                        for half in range(2):
                            near_ref[span(2 * b + half), span(2 * half)] = tap[:, 0:C]
                            near_ref[span(2 * b + half), span(2 * half + 1)] = tap[:, C:2 * C]
                for out in range(-1, 3):
                    plain_ref[b, span(in_all[out + a - 1]), span(out + 1)] = tap[:, 2 * C:3 * C]

    pl.when(core_ref[0] == 0)(lambda: place(0))
    pl.when(core_ref[0] == 1)(lambda: place(1))
    for b in range(3):
        v_ref[b] = lax.dot_general(
            plain_ref[b], order, (((1,), (1,)), ((), ())), preferred_element_type=F32
        ).astype(BF)
    plain_ref[...] = jnp.zeros(plain_ref.shape, BF)
    for b in range(3):
        for a in range(3):
            for out in range(2):
                plain_ref[b, span(out + a), span(out)] = wo_ref[3 * a + b]
        o_ref[b] = jnp.dot(order, plain_ref[b, :4 * C, :2 * C], preferred_element_type=F32).astype(BF)


def params():
    return pltpu.CompilerParams(vmem_limit_bytes=VMEM_LIMIT)


def cost(flops, moved):
    return pl.CostEstimate(flops=flops, bytes_accessed=moved, transcendentals=0)


def place_weights(core, w_qkv, w_out):
    vmem = pl.BlockSpec(memory_space=pltpu.VMEM)
    return pl.pallas_call(
        place_weights_kernel,
        in_specs=[pl.BlockSpec(memory_space=pltpu.SMEM), vmem, vmem],
        out_shape=(
            jax.ShapeDtypeStruct((3, 4 * C, 4 * C), BF),
            jax.ShapeDtypeStruct((6 * C, 4 * C), BF),
            jax.ShapeDtypeStruct((3, 6 * C, 4 * C), BF),
            jax.ShapeDtypeStruct((3, 4 * C, 2 * C), BF),
        ),
        scratch_shapes=[pltpu.VMEM((3, 6 * C, 4 * C), BF)],
        compiler_params=params(),
        cost_estimate=cost(0, 1500000),
    )(core.reshape(1), jnp.swapaxes(w_qkv, 1, 2), jnp.swapaxes(w_out, 1, 2))


def windows_kernel(rows_ref, out_ref, cells_ref):
    members = rows_ref.shape[0]
    edge = 2 * members
    cells_ref[:edge] = jnp.zeros((edge, LANES), F32)
    cells_ref[edge + LON * members:] = jnp.zeros((edge, LANES), F32)
    for m in range(members):
        cells_ref[pl.ds(edge + m, LON, stride=members)] = rows_ref[m].astype(F32).T
    for g in range(GROUPS):
        start = g * LB * members
        out_ref[g] = cells_ref[start:start + LW * members].astype(BF)


def windows_of(rows):
    members = rows.shape[0]
    return pl.pallas_call(
        windows_kernel,
        out_shape=jax.ShapeDtypeStruct((GROUPS, LW * members, LANES), BF),
        scratch_shapes=[pltpu.VMEM(((LON + 4) * members, LANES), F32)],
        compiler_params=params(),
        cost_estimate=cost(0, 1700000),
    )(rows)


def pack_kernel(row_ref, own_ref, packed_ref):
    for row in range(ROWS):
        lanes = slice(row * C, (row + 1) * C)

        @pl.when(row_ref[0] == row)
        def _():
            packed_ref[...] = jnp.concatenate([own_ref[:PACK, :, lanes], own_ref[LW - PACK:, :, lanes]], axis=-1)


def pack(row, own):
    return pl.pallas_call(
        pack_kernel,
        in_specs=[pl.BlockSpec(memory_space=pltpu.SMEM), pl.BlockSpec(memory_space=pltpu.VMEM)],
        out_shape=jax.ShapeDtypeStruct((PACK, M, LANES), BF),
        compiler_params=params(),
        cost_estimate=cost(0, 1300000),
    )(row.reshape(1), own)


def conv_rows(x, w_ref, count):
    total = None
    for b in range(3):
        part = jnp.dot(x[b:b + count].reshape(count * M, x.shape[-1]), w_ref[b], preferred_element_type=F32)
        total = part if total is None else total + part
    return total


def head_masks(lanes):
    lane = lax.broadcasted_iota(jnp.int32, (1, lanes), 1)
    head = (lane % C) // HD
    return [(head == h).astype(BF) for h in range(HEADS)]


def score_step(qk, count):
    masks = head_masks(LANES)
    q = jnp.concatenate([qk[l, :, :C] for l in range(count)], axis=-1)
    k = jnp.concatenate([qk[l, :, C:] for l in range(count)], axis=-1)
    pairs = [k[:, i * LANES:(i + 1) * LANES] for i in range(count // 2)]
    km = jnp.concatenate([jnp.concatenate([p * mask for p in pairs], axis=-1) for mask in masks], axis=0)
    return lax.dot_general(q, km, (((1,), (1,)), ((), ())), preferred_element_type=F32)


def score_step_by_half(qk, count):
    lane = lax.broadcasted_iota(jnp.int32, (1, LANES), 1)
    masks = [(lane % (C // 2) // HD == h).astype(BF) for h in range(HEADS // 2)]
    parts = []
    for start in (0, C // 2):
        q = jnp.concatenate([qk[l, :, start:start + C // 2] for l in range(count)], axis=-1)
        k = jnp.concatenate([qk[l, :, C + start:C + start + C // 2] for l in range(count)], axis=-1)
        tiles = [k[:, i * LANES:(i + 1) * LANES] for i in range(count // 4)]
        km = jnp.concatenate([jnp.concatenate([t * mask for t in tiles], axis=-1) for mask in masks], axis=0)
        parts.append(lax.dot_general(q, km, (((1,), (1,)), ((), ())), preferred_element_type=F32))
    return jnp.concatenate(parts, axis=-1)


def early_kernel(mate_ref, own_ref, w_ref, s_ref, late_ref):
    step, joined = 8, 3
    total = None
    held = []
    for start in range(0, LB, step):
        window = slice(start + 1, start + step + 3)
        x = jnp.concatenate([mate_ref[window], own_ref[window]], axis=-1)
        qk = conv_rows(x, w_ref, step)
        late_ref[start:start + step] = qk[:, LANES:].reshape(step, M, LANES)
        held.append(qk[:, :LANES].astype(BF).reshape(step, M, LANES))
        if len(held) == joined:
            part = score_step(jnp.concatenate(held, axis=0), step * joined)
            total = part if total is None else total + part
            held = []
    s_ref[...] = total


def late_kernel(near_ref, late_ref, first_ref, w_ref, s_ref, near_out, sems):
    copy = pltpu.make_async_copy(near_ref, near_out, sems.at[0])
    copy.start()
    step = 6
    total = first_ref[...]
    for start in range(0, HALF, step):
        x = jnp.concatenate([near_ref[start + 1 + b:start + 1 + b + step] for b in range(3)], axis=-1)
        add = jnp.dot(x.reshape(step * M, 6 * C), w_ref[...], preferred_element_type=F32)
        halves = []
        for half in range(2):
            at = half * HALF + start
            qk = late_ref[at:at + step].reshape(step * M, LANES) + add[:, half * LANES:(half + 1) * LANES]
            halves.append(qk.astype(BF).reshape(step, M, LANES))
        total = total + score_step_by_half(jnp.concatenate(halves, axis=0), 2 * step)
    for a in range(M // 8):
        for b in range(HEADS * M // 128):
            s_ref[a * (HEADS * M // 128) + b] = total[8 * a:8 * (a + 1), 128 * b:128 * (b + 1)]
    copy.wait()


def early_scores(mate, own, w_qk):
    return pl.pallas_call(
        early_kernel,
        out_shape=(jax.ShapeDtypeStruct((M, HEADS * M), F32), jax.ShapeDtypeStruct((LB, M, LANES), F32)),
        compiler_params=params(),
        cost_estimate=cost(3_000_000_000, 3000000),
    )(mate, own, w_qk)


def late_scores(near, late, first, w_near):
    tiles = HEADS * M * M // 1024
    return pl.pallas_call(
        late_kernel,
        out_shape=(jax.ShapeDtypeStruct((tiles, 8, 128), F32), pltpu.HBM(near.shape, BF)),
        out_specs=(pl.BlockSpec(memory_space=pltpu.VMEM), pl.BlockSpec(memory_space=pltpu.HBM)),
        scratch_shapes=[pltpu.SemaphoreType.DMA((1,))],
        compiler_params=params(),
        cost_estimate=cost(2_000_000_000, 3000000),
    )(near, late, first, w_near)


def values_kernel(near_in, far_in, own_ref, mate_ref, w_ref, keep_ref, held_ref, v_out, near_ref, far_ref, x_ref, v_ref, sems):
    arriving = [
        pltpu.make_async_copy(near_in, near_ref, sems.at[5]),
        pltpu.make_async_copy(far_in, far_ref, sems.at[6]),
    ]
    for copy in arriving:
        copy.start()
    for copy in arriving:
        copy.wait()
    half = LW // 2
    skip = half - (LW - PACK)
    x_ref[:half, :, :LANES] = jnp.concatenate([near_ref[:half, :, :C], far_ref[:half, :, :C]], axis=-1)
    x_ref[half:, :, :LANES] = jnp.concatenate([near_ref[skip:, :, C:], far_ref[skip:, :, C:]], axis=-1)
    step = 10
    w = w_ref[...].reshape(18 * C, 4 * C)
    copies = []
    for start in range(0, LV, step):
        x = jnp.concatenate(
            [ref[start + b:start + b + step] for b in range(3) for ref in (x_ref, own_ref, mate_ref)], axis=-1
        )
        v = jnp.dot(x.reshape(step * M, 18 * C), w, preferred_element_type=F32)
        v = (v.reshape(step, M, 4 * C) * keep_ref[start:start + step]).astype(BF)
        if start < HELD:
            held_ref[start:start + step] = v
        else:
            piece = slice(start - HELD, start - HELD + step)
            v_ref[piece] = v
            copies.append(pltpu.make_async_copy(v_ref.at[piece], v_out.at[piece], sems.at[start // step]))
            copies[-1].start()
    for copy in copies:
        copy.wait()


def value_maps(near, far, own, mate, w_v, keep):
    vmem = pl.BlockSpec(memory_space=pltpu.VMEM)
    hbm = pl.BlockSpec(memory_space=pltpu.HBM)
    return pl.pallas_call(
        values_kernel,
        in_specs=[hbm, hbm, vmem, vmem, vmem, vmem],
        out_shape=(jax.ShapeDtypeStruct((HELD, M, 4 * C), BF), pltpu.HBM((LV - HELD, M, 4 * C), BF)),
        out_specs=(vmem, hbm),
        scratch_shapes=[
            pltpu.VMEM((PACK, M, LANES), BF),
            pltpu.VMEM((PACK, M, LANES), BF),
            pltpu.VMEM((LW, M, LANES), BF),
            pltpu.VMEM((LV - HELD, M, 4 * C), BF),
            pltpu.SemaphoreType.DMA((7,)),
        ],
        compiler_params=params(),
        cost_estimate=cost(2_000_000_000, 4000000),
    )(pltpu.with_memory_space_constraint(near, pltpu.HBM), pltpu.with_memory_space_constraint(far, pltpu.HBM), own, mate, w_v, keep)


def mix_kernel(attn_ref, held_ref, v_in, own_ref, w_ref, out_ref, v_ref, att_ref, sems):
    copy = pltpu.make_async_copy(v_in, v_ref, sems.at[0])
    copy.start()
    lane = lax.broadcasted_iota(jnp.int32, (1, 4 * C), 1) % LANES
    masks = [(lane // (4 * HD) == h).astype(BF) for h in range(HEADS // 2)]
    lane_tiles = HEADS * M // 128
    attn = jnp.concatenate(
        [jnp.concatenate([attn_ref[a * lane_tiles + b] for b in range(lane_tiles)], axis=-1) for a in range(M // 8)],
        axis=0,
    )
    for first, ref in ((0, held_ref), (HELD, v_ref)):
        if first:
            copy.wait()
        for i in range(0, ref.shape[0], 2):
            t = first + i
            for half in range(2):
                lanes = slice(half * LANES, (half + 1) * LANES)
                v = jnp.concatenate([ref[i, :, lanes], ref[i + 1, :, lanes]], axis=-1)
                vm = jnp.concatenate([v * mask for mask in masks], axis=0)
                weights = attn[:, half * 4 * M:(half + 1) * 4 * M]
                blended = jnp.dot(weights, vm, preferred_element_type=F32).astype(BF)
                att_ref[t, :, lanes] = blended[:, :LANES]
                att_ref[t + 1, :, lanes] = blended[:, LANES:]
    step = 8
    for start in range(0, LB, step):
        total = own_ref[start + 2:start + 2 + step].astype(F32).reshape(step * M, LANES)
        for b in range(3):
            x = att_ref[start + b:start + b + step].reshape(step * M, 4 * C)
            total = total + jnp.dot(x, w_ref[b], preferred_element_type=F32)
        out_ref[start:start + step] = total.astype(BF).reshape(step, M, LANES)


def mix(attn, held, v, own, w_o):
    vmem = pl.BlockSpec(memory_space=pltpu.VMEM)
    hbm = pl.BlockSpec(memory_space=pltpu.HBM)
    return pl.pallas_call(
        mix_kernel,
        in_specs=[vmem, vmem, hbm, vmem, vmem],
        out_shape=jax.ShapeDtypeStruct((LB, M, LANES), BF),
        scratch_shapes=[
            pltpu.VMEM((LV - HELD, M, 4 * C), BF),
            pltpu.VMEM((LV, M, 4 * C), BF),
            pltpu.SemaphoreType.DMA((1,)),
        ],
        compiler_params=params(),
        cost_estimate=cost(4_000_000_000, 4000000),
    )(attn, held, pltpu.with_memory_space_constraint(v, pltpu.HBM), own, w_o)


def total_kernel(parts_ref, out_ref):
    total = parts_ref[0]
    for i in range(1, parts_ref.shape[0]):
        total = total + parts_ref[i]
    for g in range(out_ref.shape[0]):
        out_ref[g] = total


def summed(parts, copies):
    return pl.pallas_call(
        total_kernel,
        out_shape=jax.ShapeDtypeStruct((copies,) + parts.shape[1:], F32),
        compiler_params=params(),
        cost_estimate=cost(0, 300000),
    )(parts)


def softmax_kernel(scale, parts_ref, out_ref):
    total = parts_ref[0]
    for i in range(1, parts_ref.shape[0]):
        total = total + parts_ref[i]
    total = total * scale
    low = lax.broadcasted_iota(jnp.int32, total.shape, 1) < M

    def halves(reduce, x, fill):
        first = reduce(jnp.where(low, x, fill), axis=-1, keepdims=True)
        second = reduce(jnp.where(low, fill, x), axis=-1, keepdims=True)
        return jnp.where(low, first, second)

    e = jnp.exp(total - halves(jnp.max, total, -jnp.inf))
    attn = (e / halves(jnp.sum, e, 0.0)).astype(BF)
    for g in range(out_ref.shape[0]):
        out_ref[g] = attn


def softmax_of(parts, scale, copies):
    return pl.pallas_call(
        functools.partial(softmax_kernel, scale),
        out_shape=jax.ShapeDtypeStruct((copies,) + parts.shape[1:], BF),
        compiler_params=params(),
        cost_estimate=cost(0, 300000),
    )(parts)


def row_order():
    old = lax.broadcasted_iota(jnp.int32, (LANES, LANES), 0)
    new = lax.broadcasted_iota(jnp.int32, (LANES, LANES), 1)
    return (old % ROWS * C + old // ROWS == new).astype(BF)


def final_kernel(back_ref, out_hbm, cells_ref, out_ref, sems):
    members = out_ref.shape[0]
    count = LB * members
    for g in range(GROUPS):
        cells_ref[g * count:(g + 1) * count] = back_ref[g].astype(F32)
    order = row_order()
    copies = []
    for m in range(members):
        cells = cells_ref[pl.ds(m, LON, stride=members)].astype(BF)
        rows = lax.dot_general(order, cells, (((1,), (1,)), ((), ())), preferred_element_type=F32)
        out_ref[m] = rows.astype(BF).reshape(C, ROWS, LON)
        copies.append(pltpu.make_async_copy(out_ref.at[m], out_hbm.at[m], sems.at[m]))
        copies[m].start()
    for copy in copies:
        copy.wait()


def final_layout(back):
    members = back.shape[1] // LB
    shape = (members, C, ROWS, LON)
    return pl.pallas_call(
        final_kernel,
        out_shape=jax.ShapeDtypeStruct(shape, BF),
        out_specs=pl.BlockSpec(memory_space=pl.ANY),
        scratch_shapes=[
            pltpu.VMEM((LON * members, LANES), F32),
            pltpu.VMEM(shape, BF),
            pltpu.SemaphoreType.DMA((members,)),
        ],
        compiler_params=params(),
        cost_estimate=cost(0, 1600000),
    )(back)


def local(fields, w_qkv, w_out):
    members_here = fields.shape[0]
    core = lax.axis_index("core")
    place = lax.axis_index(SPACE)
    group = lax.axis_index("mem")
    places = lax.axis_size(SPACE)
    last_place = places - 1

    rows = jnp.transpose(fields, (0, 2, 1, 3)).reshape(members_here, LANES, LON)
    windows = windows_of(rows).reshape(GROUPS, LW, members_here, LANES)
    arrived = lax.all_to_all(windows, "mem", split_axis=0, concat_axis=0, tiled=True)
    own = jnp.transpose(arrived, (1, 0, 2, 3)).reshape(LW, M, LANES)
    seams = [(i, i + 1) for i in range(1, last_place, 2)]
    seams = seams + [(j, i) for i, j in seams]
    near = lax.ppermute(pack(core, own), SPACE, seams)
    mate = lax.ppermute(own, "core", [(0, 1), (1, 0)])
    far = lax.ppermute(pack(1 - core, own), SPACE, seams)
    own, w_qkv = lax.optimization_barrier((own, w_qkv))
    w_qk, w_near, w_v, w_o = place_weights(core, w_qkv, w_out)
    first, late = early_scores(mate, own, w_qk)
    part, near = late_scores(near, late, first, w_near)

    row = lax.broadcasted_iota(jnp.int32, (LV, 1, 4 * C), 2) % (4 * HD) // HD
    lon = lax.broadcasted_iota(jnp.int32, (LV, 1, 4 * C), 0)
    outside = (
        ((row == 0) & (place == 0))
        | ((row == 3) & (place == last_place))
        | ((lon == 0) & (group == 0))
        | ((lon == LV - 1) & (group == GROUPS - 1))
    )
    keep = jnp.where(outside, 0.0, 1.0).astype(F32)
    part = lax.all_to_all(part, SPACE, split_axis=0, concat_axis=0, tiled=True)
    held, v = value_maps(near, far, own, mate, w_v, keep)
    part, held, v = lax.optimization_barrier((part, held, v))
    part = lax.all_to_all(summed(part, GROUPS), "mem", split_axis=0, concat_axis=0, tiled=True)
    attn = softmax_of(part, 1.0 / math.sqrt(HD * ROWS * places * LON), places)
    attn = lax.all_to_all(attn, SPACE, split_axis=0, concat_axis=0, tiled=True)
    mixed = mix(attn, held, v, own, w_o)
    mixed = jnp.transpose(mixed.reshape(LB, GROUPS, members_here, LANES), (1, 0, 2, 3))
    back = lax.all_to_all(mixed, "mem", split_axis=0, concat_axis=0, tiled=True)
    return final_layout(back.reshape(GROUPS, LB * members_here, LANES))


def solution(mesh):
    whole = Mesh(mesh.devices.reshape(4, 4, 2, 8), ("x", "y", "core", "mem"))
    return jax.shard_map(
        local,
        mesh=whole,
        in_specs=(P("mem", None, SPACE, None), P(), P()),
        out_specs=P("mem", None, SPACE, None),
        check_vma=False,
    )
```

```python
import functools
import math

import jax
import jax.numpy as jnp
from jax import lax
from jax.experimental import pallas as pl
from jax.experimental.pallas import tpu as pltpu
from jax.sharding import Mesh
from jax.sharding import PartitionSpec as P

C = 64
HEADS = 8
HD = 8
M = 64
ROWS = 2
LANES = ROWS * C
GROUPS = 8
LON = 384
LB = LON // GROUPS
LW = LB + 4
LV = LB + 2
HALF = LB // 2
PACK = HALF + 4
HELD = 20
SPACE = ("x", "y", "core")
BF = jnp.bfloat16
F32 = jnp.float32
VMEM_LIMIT = 24 * 1024 * 1024


def place_weights_kernel(core_ref, w_ref, wo_ref, qk_ref, near_ref, v_ref, o_ref, plain_ref):
    for ref in (qk_ref, near_ref, plain_ref):
        ref[...] = jnp.zeros(ref.shape, BF)
    new = lax.broadcasted_iota(jnp.int32, (4 * C, 4 * C), 0)
    old = lax.broadcasted_iota(jnp.int32, (4 * C, 4 * C), 1)
    wanted = new % (4 * HD) // HD * C + new // (4 * HD) * HD + new % HD
    order = (wanted == old).astype(BF)

    def span(i):
        return slice(i * C, (i + 1) * C)

    def place(core):
        early, late = 1 - core, core
        near = -1 if core == 0 else 2
        far = -2 if core == 0 else 3
        mate = 2 if core == 0 else -2
        in_pair = {mate: 0, mate + 1: 1, 0: 2, 1: 3}
        in_all = {near: 0, far: 1, 0: 2, 1: 3, mate: 4, mate + 1: 5}
        for b in range(3):
            for a in range(3):
                tap = w_ref[3 * a + b]
                for out, part in ((early, 0), (late, 2)):
                    row = out + a - 1
                    if row in in_pair:
                        qk_ref[b, span(in_pair[row]), span(part)] = tap[:, 0:C]
                        qk_ref[b, span(in_pair[row]), span(part + 1)] = tap[:, C:2 * C]
                    else:
                        for half in range(2):
                            near_ref[span(2 * b + half), span(2 * half)] = tap[:, 0:C]
                            near_ref[span(2 * b + half), span(2 * half + 1)] = tap[:, C:2 * C]
                for out in range(-1, 3):
                    plain_ref[b, span(in_all[out + a - 1]), span(out + 1)] = tap[:, 2 * C:3 * C]

    pl.when(core_ref[0] == 0)(lambda: place(0))
    pl.when(core_ref[0] == 1)(lambda: place(1))
    for b in range(3):
        v_ref[b] = lax.dot_general(
            plain_ref[b], order, (((1,), (1,)), ((), ())), preferred_element_type=F32
        ).astype(BF)
    plain_ref[...] = jnp.zeros(plain_ref.shape, BF)
    for b in range(3):
        for a in range(3):
            for out in range(2):
                plain_ref[b, span(out + a), span(out)] = wo_ref[3 * a + b]
        o_ref[b] = jnp.dot(order, plain_ref[b, :4 * C, :2 * C], preferred_element_type=F32).astype(BF)


def params():
    return pltpu.CompilerParams(vmem_limit_bytes=VMEM_LIMIT)


def cost(flops, moved):
    return pl.CostEstimate(flops=flops, bytes_accessed=moved, transcendentals=0)


def place_weights(core, w_qkv, w_out):
    vmem = pl.BlockSpec(memory_space=pltpu.VMEM)
    return pl.pallas_call(
        place_weights_kernel,
        in_specs=[pl.BlockSpec(memory_space=pltpu.SMEM), vmem, vmem],
        out_shape=(
            jax.ShapeDtypeStruct((3, 4 * C, 4 * C), BF),
            jax.ShapeDtypeStruct((6 * C, 4 * C), BF),
            jax.ShapeDtypeStruct((3, 6 * C, 4 * C), BF),
            jax.ShapeDtypeStruct((3, 4 * C, 2 * C), BF),
        ),
        scratch_shapes=[pltpu.VMEM((3, 6 * C, 4 * C), BF)],
        compiler_params=params(),
        cost_estimate=cost(0, 1500000),
    )(core.reshape(1), jnp.swapaxes(w_qkv, 1, 2), jnp.swapaxes(w_out, 1, 2))


def windows_kernel(rows_ref, out_ref, cells_ref):
    members = rows_ref.shape[0]
    edge = 2 * members
    cells_ref[:edge] = jnp.zeros((edge, LANES), F32)
    cells_ref[edge + LON * members:] = jnp.zeros((edge, LANES), F32)
    for m in range(members):
        cells_ref[pl.ds(edge + m, LON, stride=members)] = rows_ref[m].astype(F32).T
    for g in range(GROUPS):
        start = g * LB * members
        out_ref[g] = cells_ref[start:start + LW * members].astype(BF)


def windows_of(rows):
    members = rows.shape[0]
    return pl.pallas_call(
        windows_kernel,
        out_shape=jax.ShapeDtypeStruct((GROUPS, LW * members, LANES), BF),
        scratch_shapes=[pltpu.VMEM(((LON + 4) * members, LANES), F32)],
        compiler_params=params(),
        cost_estimate=cost(0, 1700000),
    )(rows)


def pack_kernel(row_ref, own_ref, packed_ref):
    for row in range(ROWS):
        lanes = slice(row * C, (row + 1) * C)

        @pl.when(row_ref[0] == row)
        def _():
            packed_ref[...] = jnp.concatenate([own_ref[:PACK, :, lanes], own_ref[LW - PACK:, :, lanes]], axis=-1)


def pack(row, own):
    return pl.pallas_call(
        pack_kernel,
        in_specs=[pl.BlockSpec(memory_space=pltpu.SMEM), pl.BlockSpec(memory_space=pltpu.VMEM)],
        out_shape=jax.ShapeDtypeStruct((PACK, M, LANES), BF),
        compiler_params=params(),
        cost_estimate=cost(0, 1300000),
    )(row.reshape(1), own)


def conv_rows(x, w_ref, count):
    total = None
    for b in range(3):
        part = jnp.dot(x[b:b + count].reshape(count * M, x.shape[-1]), w_ref[b], preferred_element_type=F32)
        total = part if total is None else total + part
    return total


def head_masks(lanes):
    lane = lax.broadcasted_iota(jnp.int32, (1, lanes), 1)
    head = (lane % C) // HD
    return [(head == h).astype(BF) for h in range(HEADS)]


def score_step(qk, count):
    masks = head_masks(LANES)
    q = jnp.concatenate([qk[l, :, :C] for l in range(count)], axis=-1)
    k = jnp.concatenate([qk[l, :, C:] for l in range(count)], axis=-1)
    pairs = [k[:, i * LANES:(i + 1) * LANES] for i in range(count // 2)]
    km = jnp.concatenate([jnp.concatenate([p * mask for p in pairs], axis=-1) for mask in masks], axis=0)
    return lax.dot_general(q, km, (((1,), (1,)), ((), ())), preferred_element_type=F32)


def score_step_by_half(qk, count):
    lane = lax.broadcasted_iota(jnp.int32, (1, LANES), 1)
    masks = [(lane % (C // 2) // HD == h).astype(BF) for h in range(HEADS // 2)]
    parts = []
    for start in (0, C // 2):
        q = jnp.concatenate([qk[l, :, start:start + C // 2] for l in range(count)], axis=-1)
        k = jnp.concatenate([qk[l, :, C + start:C + start + C // 2] for l in range(count)], axis=-1)
        tiles = [k[:, i * LANES:(i + 1) * LANES] for i in range(count // 4)]
        km = jnp.concatenate([jnp.concatenate([t * mask for t in tiles], axis=-1) for mask in masks], axis=0)
        parts.append(lax.dot_general(q, km, (((1,), (1,)), ((), ())), preferred_element_type=F32))
    return jnp.concatenate(parts, axis=-1)


def early_kernel(mate_ref, own_ref, w_ref, s_ref, late_ref):
    step, joined = 8, 3
    total = None
    held = []
    for start in range(0, LB, step):
        window = slice(start + 1, start + step + 3)
        x = jnp.concatenate([mate_ref[window], own_ref[window]], axis=-1)
        qk = conv_rows(x, w_ref, step)
        late_ref[start:start + step] = qk[:, LANES:].reshape(step, M, LANES)
        held.append(qk[:, :LANES].astype(BF).reshape(step, M, LANES))
        if len(held) == joined:
            part = score_step(jnp.concatenate(held, axis=0), step * joined)
            total = part if total is None else total + part
            held = []
    s_ref[...] = total


def late_kernel(near_ref, late_ref, first_ref, w_ref, s_ref, near_out, sems):
    copy = pltpu.make_async_copy(near_ref, near_out, sems.at[0])
    copy.start()
    step = 6
    total = first_ref[...]
    for start in range(0, HALF, step):
        x = jnp.concatenate([near_ref[start + 1 + b:start + 1 + b + step] for b in range(3)], axis=-1)
        add = jnp.dot(x.reshape(step * M, 6 * C), w_ref[...], preferred_element_type=F32)
        halves = []
        for half in range(2):
            at = half * HALF + start
            qk = late_ref[at:at + step].reshape(step * M, LANES) + add[:, half * LANES:(half + 1) * LANES]
            halves.append(qk.astype(BF).reshape(step, M, LANES))
        total = total + score_step_by_half(jnp.concatenate(halves, axis=0), 2 * step)
    for a in range(M // 8):
        for b in range(HEADS * M // 128):
            s_ref[a * (HEADS * M // 128) + b] = total[8 * a:8 * (a + 1), 128 * b:128 * (b + 1)]
    copy.wait()


def early_scores(mate, own, w_qk):
    return pl.pallas_call(
        early_kernel,
        out_shape=(jax.ShapeDtypeStruct((M, HEADS * M), F32), jax.ShapeDtypeStruct((LB, M, LANES), F32)),
        compiler_params=params(),
        cost_estimate=cost(3_000_000_000, 3000000),
    )(mate, own, w_qk)


def late_scores(near, late, first, w_near):
    tiles = HEADS * M * M // 1024
    return pl.pallas_call(
        late_kernel,
        out_shape=(jax.ShapeDtypeStruct((tiles, 8, 128), F32), pltpu.HBM(near.shape, BF)),
        out_specs=(pl.BlockSpec(memory_space=pltpu.VMEM), pl.BlockSpec(memory_space=pltpu.HBM)),
        scratch_shapes=[pltpu.SemaphoreType.DMA((1,))],
        compiler_params=params(),
        cost_estimate=cost(2_000_000_000, 3000000),
    )(near, late, first, w_near)


def values_kernel(near_in, far_in, own_ref, mate_ref, w_ref, keep_ref, held_ref, v_out, near_ref, far_ref, x_ref, v_ref, sems):
    arriving = [
        pltpu.make_async_copy(near_in, near_ref, sems.at[5]),
        pltpu.make_async_copy(far_in, far_ref, sems.at[6]),
    ]
    for copy in arriving:
        copy.start()
    step = 10
    inside = jnp.concatenate([w_ref[b, LANES:] for b in range(3)], axis=0)
    seam = jnp.concatenate([w_ref[b, :LANES] for b in range(3)], axis=0)

    def part(refs, w, start):
        x = jnp.concatenate([ref[start + b:start + b + step] for b in range(3) for ref in refs], axis=-1)
        return jnp.dot(x.reshape(step * M, w.shape[0]), w, preferred_element_type=F32)

    early = [part((own_ref, mate_ref), inside, start) for start in (0, step)]
    for copy in arriving:
        copy.wait()
    half = LW // 2
    skip = half - (LW - PACK)
    x_ref[:half] = jnp.concatenate([near_ref[:half, :, :C], far_ref[:half, :, :C]], axis=-1)
    x_ref[half:] = jnp.concatenate([near_ref[skip:, :, C:], far_ref[skip:, :, C:]], axis=-1)
    w = w_ref[...].reshape(18 * C, 4 * C)
    copies = []
    for start in range(0, LV, step):
        if start < HELD:
            v = early[start // step] + part((x_ref,), seam, start)
        else:
            v = part((x_ref, own_ref, mate_ref), w, start)
        v = (v.reshape(step, M, 4 * C) * keep_ref[start:start + step]).astype(BF)
        if start < HELD:
            held_ref[start:start + step] = v
        else:
            piece = slice(start - HELD, start - HELD + step)
            v_ref[piece] = v
            copies.append(pltpu.make_async_copy(v_ref.at[piece], v_out.at[piece], sems.at[start // step]))
            copies[-1].start()
    for copy in copies:
        copy.wait()


def value_maps(near, far, own, mate, w_v, keep):
    vmem = pl.BlockSpec(memory_space=pltpu.VMEM)
    hbm = pl.BlockSpec(memory_space=pltpu.HBM)
    return pl.pallas_call(
        values_kernel,
        in_specs=[hbm, hbm, vmem, vmem, vmem, vmem],
        out_shape=(jax.ShapeDtypeStruct((HELD, M, 4 * C), BF), pltpu.HBM((LV - HELD, M, 4 * C), BF)),
        out_specs=(vmem, hbm),
        scratch_shapes=[
            pltpu.VMEM((PACK, M, LANES), BF),
            pltpu.VMEM((PACK, M, LANES), BF),
            pltpu.VMEM((LW, M, LANES), BF),
            pltpu.VMEM((LV - HELD, M, 4 * C), BF),
            pltpu.SemaphoreType.DMA((7,)),
        ],
        compiler_params=params(),
        cost_estimate=cost(2_000_000_000, 4000000),
    )(pltpu.with_memory_space_constraint(near, pltpu.HBM), pltpu.with_memory_space_constraint(far, pltpu.HBM), own, mate, w_v, keep)


def mix_kernel(attn_ref, held_ref, v_in, own_ref, w_ref, out_ref, v_ref, att_ref, sems):
    copy = pltpu.make_async_copy(v_in, v_ref, sems.at[0])
    copy.start()
    lane = lax.broadcasted_iota(jnp.int32, (1, 4 * C), 1) % LANES
    masks = [(lane // (4 * HD) == h).astype(BF) for h in range(HEADS // 2)]
    lane_tiles = HEADS * M // 128
    attn = jnp.concatenate(
        [jnp.concatenate([attn_ref[a * lane_tiles + b] for b in range(lane_tiles)], axis=-1) for a in range(M // 8)],
        axis=0,
    )
    for first, ref in ((0, held_ref), (HELD, v_ref)):
        if first:
            copy.wait()
        for i in range(0, ref.shape[0], 2):
            t = first + i
            for half in range(2):
                lanes = slice(half * LANES, (half + 1) * LANES)
                v = jnp.concatenate([ref[i, :, lanes], ref[i + 1, :, lanes]], axis=-1)
                vm = jnp.concatenate([v * mask for mask in masks], axis=0)
                weights = attn[:, half * 4 * M:(half + 1) * 4 * M]
                blended = jnp.dot(weights, vm, preferred_element_type=F32).astype(BF)
                att_ref[t, :, lanes] = blended[:, :LANES]
                att_ref[t + 1, :, lanes] = blended[:, LANES:]
    step = 8
    for start in range(0, LB, step):
        total = own_ref[start + 2:start + 2 + step].astype(F32).reshape(step * M, LANES)
        for b in range(3):
            x = att_ref[start + b:start + b + step].reshape(step * M, 4 * C)
            total = total + jnp.dot(x, w_ref[b], preferred_element_type=F32)
        out_ref[start:start + step] = total.astype(BF).reshape(step, M, LANES)


def mix(attn, held, v, own, w_o):
    vmem = pl.BlockSpec(memory_space=pltpu.VMEM)
    hbm = pl.BlockSpec(memory_space=pltpu.HBM)
    return pl.pallas_call(
        mix_kernel,
        in_specs=[vmem, vmem, hbm, vmem, vmem],
        out_shape=jax.ShapeDtypeStruct((LB, M, LANES), BF),
        scratch_shapes=[
            pltpu.VMEM((LV - HELD, M, 4 * C), BF),
            pltpu.VMEM((LV, M, 4 * C), BF),
            pltpu.SemaphoreType.DMA((1,)),
        ],
        compiler_params=params(),
        cost_estimate=cost(4_000_000_000, 4000000),
    )(attn, held, pltpu.with_memory_space_constraint(v, pltpu.HBM), own, w_o)


def total_kernel(parts_ref, out_ref):
    total = parts_ref[0]
    for i in range(1, parts_ref.shape[0]):
        total = total + parts_ref[i]
    for g in range(out_ref.shape[0]):
        out_ref[g] = total


def summed(parts, copies):
    return pl.pallas_call(
        total_kernel,
        out_shape=jax.ShapeDtypeStruct((copies,) + parts.shape[1:], F32),
        compiler_params=params(),
        cost_estimate=cost(0, 300000),
    )(parts)


def softmax_kernel(scale, parts_ref, out_ref):
    total = parts_ref[0]
    for i in range(1, parts_ref.shape[0]):
        total = total + parts_ref[i]
    total = total * scale
    low = lax.broadcasted_iota(jnp.int32, total.shape, 1) < M

    def halves(reduce, x, fill):
        first = reduce(jnp.where(low, x, fill), axis=-1, keepdims=True)
        second = reduce(jnp.where(low, fill, x), axis=-1, keepdims=True)
        return jnp.where(low, first, second)

    e = jnp.exp(total - halves(jnp.max, total, -jnp.inf))
    attn = (e / halves(jnp.sum, e, 0.0)).astype(BF)
    for g in range(out_ref.shape[0]):
        out_ref[g] = attn


def softmax_of(parts, scale, copies):
    return pl.pallas_call(
        functools.partial(softmax_kernel, scale),
        out_shape=jax.ShapeDtypeStruct((copies,) + parts.shape[1:], BF),
        compiler_params=params(),
        cost_estimate=cost(0, 300000),
    )(parts)


def row_order():
    old = lax.broadcasted_iota(jnp.int32, (LANES, LANES), 0)
    new = lax.broadcasted_iota(jnp.int32, (LANES, LANES), 1)
    return (old % ROWS * C + old // ROWS == new).astype(BF)


def final_kernel(back_ref, out_hbm, cells_ref, out_ref, sems):
    members = out_ref.shape[0]
    count = LB * members
    for g in range(GROUPS):
        cells_ref[g * count:(g + 1) * count] = back_ref[g].astype(F32)
    order = row_order()
    copies = []
    for m in range(members):
        cells = cells_ref[pl.ds(m, LON, stride=members)].astype(BF)
        rows = lax.dot_general(order, cells, (((1,), (1,)), ((), ())), preferred_element_type=F32)
        out_ref[m] = rows.astype(BF).reshape(C, ROWS, LON)
        copies.append(pltpu.make_async_copy(out_ref.at[m], out_hbm.at[m], sems.at[m]))
        copies[m].start()
    for copy in copies:
        copy.wait()


def final_layout(back):
    members = back.shape[1] // LB
    shape = (members, C, ROWS, LON)
    return pl.pallas_call(
        final_kernel,
        out_shape=jax.ShapeDtypeStruct(shape, BF),
        out_specs=pl.BlockSpec(memory_space=pl.ANY),
        scratch_shapes=[
            pltpu.VMEM((LON * members, LANES), F32),
            pltpu.VMEM(shape, BF),
            pltpu.SemaphoreType.DMA((members,)),
        ],
        compiler_params=params(),
        cost_estimate=cost(0, 1600000),
    )(back)


def local(fields, w_qkv, w_out):
    members_here = fields.shape[0]
    core = lax.axis_index("core")
    place = lax.axis_index(SPACE)
    group = lax.axis_index("mem")
    places = lax.axis_size(SPACE)
    last_place = places - 1

    rows = jnp.transpose(fields, (0, 2, 1, 3)).reshape(members_here, LANES, LON)
    windows = windows_of(rows).reshape(GROUPS, LW, members_here, LANES)
    arrived = lax.all_to_all(windows, "mem", split_axis=0, concat_axis=0, tiled=True)
    own = jnp.transpose(arrived, (1, 0, 2, 3)).reshape(LW, M, LANES)
    seams = [(i, i + 1) for i in range(1, last_place, 2)]
    seams = seams + [(j, i) for i, j in seams]
    near = lax.ppermute(pack(core, own), SPACE, seams)
    mate = lax.ppermute(own, "core", [(0, 1), (1, 0)])
    far = lax.ppermute(pack(1 - core, own), SPACE, seams)
    own, w_qkv = lax.optimization_barrier((own, w_qkv))
    w_qk, w_near, w_v, w_o = place_weights(core, w_qkv, w_out)
    first, late = early_scores(mate, own, w_qk)
    part, near = late_scores(near, late, first, w_near)

    row = lax.broadcasted_iota(jnp.int32, (LV, 1, 4 * C), 2) % (4 * HD) // HD
    lon = lax.broadcasted_iota(jnp.int32, (LV, 1, 4 * C), 0)
    outside = (
        ((row == 0) & (place == 0))
        | ((row == 3) & (place == last_place))
        | ((lon == 0) & (group == 0))
        | ((lon == LV - 1) & (group == GROUPS - 1))
    )
    keep = jnp.where(outside, 0.0, 1.0).astype(F32)
    part = lax.all_to_all(part, SPACE, split_axis=0, concat_axis=0, tiled=True)
    held, v = value_maps(near, far, own, mate, w_v, keep)
    part, held, v = lax.optimization_barrier((part, held, v))
    part = lax.all_to_all(summed(part, GROUPS), "mem", split_axis=0, concat_axis=0, tiled=True)
    attn = softmax_of(part, 1.0 / math.sqrt(HD * ROWS * places * LON), places)
    attn = lax.all_to_all(attn, SPACE, split_axis=0, concat_axis=0, tiled=True)
    mixed = mix(attn, held, v, own, w_o)
    mixed = jnp.transpose(mixed.reshape(LB, GROUPS, members_here, LANES), (1, 0, 2, 3))
    back = lax.all_to_all(mixed, "mem", split_axis=0, concat_axis=0, tiled=True)
    return final_layout(back.reshape(GROUPS, LB * members_here, LANES))


def solution(mesh):
    whole = Mesh(mesh.devices.reshape(4, 4, 2, 8), ("x", "y", "core", "mem"))
    return jax.shard_map(
        local,
        mesh=whole,
        in_specs=(P("mem", None, SPACE, None), P(), P()),
        out_specs=P("mem", None, SPACE, None),
        check_vma=False,
    )
```

```python
import functools
import math

import jax
import jax.numpy as jnp
from jax import lax
from jax.experimental import pallas as pl
from jax.experimental.pallas import tpu as pltpu
from jax.sharding import Mesh
from jax.sharding import PartitionSpec as P

C = 64
HEADS = 8
HD = 8
M = 64
ROWS = 2
LANES = ROWS * C
GROUPS = 8
LON = 384
LB = LON // GROUPS
LW = LB + 4
LV = LB + 2
HALF = LB // 2
PACK = HALF + 4
HELD = 20
SPACE = ("x", "y", "core")
BF = jnp.bfloat16
F32 = jnp.float32
VMEM_LIMIT = 16 * 1024 * 1024


def place_weights_kernel(core_ref, w_ref, wo_ref, qk_ref, near_ref, v_ref, o_ref, plain_ref):
    for ref in (qk_ref, near_ref, plain_ref):
        ref[...] = jnp.zeros(ref.shape, BF)
    new = lax.broadcasted_iota(jnp.int32, (4 * C, 4 * C), 0)
    old = lax.broadcasted_iota(jnp.int32, (4 * C, 4 * C), 1)
    wanted = new % (4 * HD) // HD * C + new // (4 * HD) * HD + new % HD
    order = (wanted == old).astype(BF)

    def span(i):
        return slice(i * C, (i + 1) * C)

    def place(core):
        early, late = 1 - core, core
        near = -1 if core == 0 else 2
        far = -2 if core == 0 else 3
        mate = 2 if core == 0 else -2
        in_pair = {mate: 0, mate + 1: 1, 0: 2, 1: 3}
        in_all = {near: 0, far: 1, 0: 2, 1: 3, mate: 4, mate + 1: 5}
        for b in range(3):
            for a in range(3):
                tap = w_ref[3 * a + b]
                for out, part in ((early, 0), (late, 2)):
                    row = out + a - 1
                    if row in in_pair:
                        qk_ref[b, span(in_pair[row]), span(part)] = tap[:, 0:C]
                        qk_ref[b, span(in_pair[row]), span(part + 1)] = tap[:, C:2 * C]
                    else:
                        for half in range(2):
                            near_ref[span(2 * b + half), span(2 * half)] = tap[:, 0:C]
                            near_ref[span(2 * b + half), span(2 * half + 1)] = tap[:, C:2 * C]
                for out in range(-1, 3):
                    plain_ref[b, span(in_all[out + a - 1]), span(out + 1)] = tap[:, 2 * C:3 * C]

    pl.when(core_ref[0] == 0)(lambda: place(0))
    pl.when(core_ref[0] == 1)(lambda: place(1))
    for b in range(3):
        v_ref[b] = lax.dot_general(
            plain_ref[b], order, (((1,), (1,)), ((), ())), preferred_element_type=F32
        ).astype(BF)
    plain_ref[...] = jnp.zeros(plain_ref.shape, BF)
    for b in range(3):
        for a in range(3):
            for out in range(2):
                plain_ref[b, span(out + a), span(out)] = wo_ref[3 * a + b]
        o_ref[b] = jnp.dot(order, plain_ref[b, :4 * C, :2 * C], preferred_element_type=F32).astype(BF)


def params():
    return pltpu.CompilerParams(vmem_limit_bytes=VMEM_LIMIT)


def cost(flops, moved):
    return pl.CostEstimate(flops=flops, bytes_accessed=moved, transcendentals=0)


def place_weights(core, w_qkv, w_out):
    vmem = pl.BlockSpec(memory_space=pltpu.VMEM)
    return pl.pallas_call(
        place_weights_kernel,
        in_specs=[pl.BlockSpec(memory_space=pltpu.SMEM), vmem, vmem],
        out_shape=(
            jax.ShapeDtypeStruct((3, 4 * C, 4 * C), BF),
            jax.ShapeDtypeStruct((6 * C, 4 * C), BF),
            jax.ShapeDtypeStruct((3, 6 * C, 4 * C), BF),
            jax.ShapeDtypeStruct((3, 4 * C, 2 * C), BF),
        ),
        scratch_shapes=[pltpu.VMEM((3, 6 * C, 4 * C), BF)],
        compiler_params=params(),
        cost_estimate=cost(0, 1500000),
    )(core.reshape(1), jnp.swapaxes(w_qkv, 1, 2), jnp.swapaxes(w_out, 1, 2))


def windows_kernel(rows_ref, out_ref, cells_ref):
    members = rows_ref.shape[0]
    edge = 2 * members
    cells_ref[:edge] = jnp.zeros((edge, LANES), F32)
    cells_ref[edge + LON * members:] = jnp.zeros((edge, LANES), F32)
    for m in range(members):
        cells_ref[pl.ds(edge + m, LON, stride=members)] = rows_ref[m].astype(F32).T
    for g in range(GROUPS):
        start = g * LB * members
        out_ref[g] = cells_ref[start:start + LW * members].astype(BF)


def windows_of(rows):
    members = rows.shape[0]
    return pl.pallas_call(
        windows_kernel,
        out_shape=jax.ShapeDtypeStruct((GROUPS, LW * members, LANES), BF),
        scratch_shapes=[pltpu.VMEM(((LON + 4) * members, LANES), F32)],
        compiler_params=params(),
        cost_estimate=cost(0, 1700000),
    )(rows)


def pack_kernel(row_ref, own_ref, packed_ref):
    for row in range(ROWS):
        lanes = slice(row * C, (row + 1) * C)

        @pl.when(row_ref[0] == row)
        def _():
            packed_ref[...] = jnp.concatenate([own_ref[:PACK, :, lanes], own_ref[LW - PACK:, :, lanes]], axis=-1)


def pack(row, own):
    return pl.pallas_call(
        pack_kernel,
        in_specs=[pl.BlockSpec(memory_space=pltpu.SMEM), pl.BlockSpec(memory_space=pltpu.VMEM)],
        out_shape=jax.ShapeDtypeStruct((PACK, M, LANES), BF),
        compiler_params=params(),
        cost_estimate=cost(0, 1300000),
    )(row.reshape(1), own)


def conv_rows(x, w_ref, count):
    total = None
    for b in range(3):
        part = jnp.dot(x[b:b + count].reshape(count * M, x.shape[-1]), w_ref[b], preferred_element_type=F32)
        total = part if total is None else total + part
    return total


def head_masks(lanes):
    lane = lax.broadcasted_iota(jnp.int32, (1, lanes), 1)
    head = (lane % C) // HD
    return [(head == h).astype(BF) for h in range(HEADS)]


def score_step(qk, count):
    masks = head_masks(LANES)
    q = jnp.concatenate([qk[l, :, :C] for l in range(count)], axis=-1)
    k = jnp.concatenate([qk[l, :, C:] for l in range(count)], axis=-1)
    pairs = [k[:, i * LANES:(i + 1) * LANES] for i in range(count // 2)]
    km = jnp.concatenate([jnp.concatenate([p * mask for p in pairs], axis=-1) for mask in masks], axis=0)
    return lax.dot_general(q, km, (((1,), (1,)), ((), ())), preferred_element_type=F32)


def score_step_by_half(qk, count):
    lane = lax.broadcasted_iota(jnp.int32, (1, LANES), 1)
    masks = [(lane % (C // 2) // HD == h).astype(BF) for h in range(HEADS // 2)]
    parts = []
    for start in (0, C // 2):
        q = jnp.concatenate([qk[l, :, start:start + C // 2] for l in range(count)], axis=-1)
        k = jnp.concatenate([qk[l, :, C + start:C + start + C // 2] for l in range(count)], axis=-1)
        tiles = [k[:, i * LANES:(i + 1) * LANES] for i in range(count // 4)]
        km = jnp.concatenate([jnp.concatenate([t * mask for t in tiles], axis=-1) for mask in masks], axis=0)
        parts.append(lax.dot_general(q, km, (((1,), (1,)), ((), ())), preferred_element_type=F32))
    return jnp.concatenate(parts, axis=-1)


def early_kernel(mate_ref, own_ref, w_ref, s_ref, late_ref):
    step, joined = 8, 3
    total = None
    held = []
    for start in range(0, LB, step):
        window = slice(start + 1, start + step + 3)
        x = jnp.concatenate([mate_ref[window], own_ref[window]], axis=-1)
        qk = conv_rows(x, w_ref, step)
        late_ref[start:start + step] = qk[:, LANES:].reshape(step, M, LANES)
        held.append(qk[:, :LANES].astype(BF).reshape(step, M, LANES))
        if len(held) == joined:
            part = score_step(jnp.concatenate(held, axis=0), step * joined)
            total = part if total is None else total + part
            held = []
    s_ref[...] = total


def late_kernel(near_ref, late_ref, first_ref, w_ref, s_ref, near_out, sems):
    copy = pltpu.make_async_copy(near_ref, near_out, sems.at[0])
    copy.start()
    step = 6
    total = first_ref[...]
    for start in range(0, HALF, step):
        x = jnp.concatenate([near_ref[start + 1 + b:start + 1 + b + step] for b in range(3)], axis=-1)
        add = jnp.dot(x.reshape(step * M, 6 * C), w_ref[...], preferred_element_type=F32)
        halves = []
        for half in range(2):
            at = half * HALF + start
            qk = late_ref[at:at + step].reshape(step * M, LANES) + add[:, half * LANES:(half + 1) * LANES]
            halves.append(qk.astype(BF).reshape(step, M, LANES))
        total = total + score_step_by_half(jnp.concatenate(halves, axis=0), 2 * step)
    for a in range(M // 8):
        for b in range(HEADS * M // 128):
            s_ref[a * (HEADS * M // 128) + b] = total[8 * a:8 * (a + 1), 128 * b:128 * (b + 1)]
    copy.wait()


def early_scores(mate, own, w_qk):
    return pl.pallas_call(
        early_kernel,
        out_shape=(jax.ShapeDtypeStruct((M, HEADS * M), F32), jax.ShapeDtypeStruct((LB, M, LANES), F32)),
        compiler_params=params(),
        cost_estimate=cost(3_000_000_000, 3000000),
    )(mate, own, w_qk)


def late_scores(near, late, first, w_near):
    tiles = HEADS * M * M // 1024
    return pl.pallas_call(
        late_kernel,
        out_shape=(jax.ShapeDtypeStruct((tiles, 8, 128), F32), pltpu.HBM(near.shape, BF)),
        out_specs=(pl.BlockSpec(memory_space=pltpu.VMEM), pl.BlockSpec(memory_space=pltpu.HBM)),
        scratch_shapes=[pltpu.SemaphoreType.DMA((1,))],
        compiler_params=params(),
        cost_estimate=cost(2_000_000_000, 3000000),
    )(near, late, first, w_near)


def values_kernel(near_in, far_in, own_ref, mate_ref, w_ref, keep_ref, held_ref, v_out, near_ref, far_ref, x_ref, v_ref, sems):
    arriving = [
        pltpu.make_async_copy(near_in, near_ref, sems.at[5]),
        pltpu.make_async_copy(far_in, far_ref, sems.at[6]),
    ]
    for copy in arriving:
        copy.start()
    for copy in arriving:
        copy.wait()
    half = LW // 2
    skip = half - (LW - PACK)
    x_ref[:half, :, :LANES] = jnp.concatenate([near_ref[:half, :, :C], far_ref[:half, :, :C]], axis=-1)
    x_ref[half:, :, :LANES] = jnp.concatenate([near_ref[skip:, :, C:], far_ref[skip:, :, C:]], axis=-1)
    step = 10
    w = w_ref[...].reshape(18 * C, 4 * C)
    copies = []
    for start in range(0, LV, step):
        x = jnp.concatenate(
            [ref[start + b:start + b + step] for b in range(3) for ref in (x_ref, own_ref, mate_ref)], axis=-1
        )
        v = jnp.dot(x.reshape(step * M, 18 * C), w, preferred_element_type=F32)
        v = (v.reshape(step, M, 4 * C) * keep_ref[start:start + step]).astype(BF)
        if start < HELD:
            held_ref[start:start + step] = v
        else:
            piece = slice(start - HELD, start - HELD + step)
            v_ref[piece] = v
            copies.append(pltpu.make_async_copy(v_ref.at[piece], v_out.at[piece], sems.at[start // step]))
            copies[-1].start()
    for copy in copies:
        copy.wait()


def value_maps(near, far, own, mate, w_v, keep):
    vmem = pl.BlockSpec(memory_space=pltpu.VMEM)
    hbm = pl.BlockSpec(memory_space=pltpu.HBM)
    return pl.pallas_call(
        values_kernel,
        in_specs=[hbm, hbm, vmem, vmem, vmem, vmem],
        out_shape=(jax.ShapeDtypeStruct((HELD, M, 4 * C), BF), pltpu.HBM((LV - HELD, M, 4 * C), BF)),
        out_specs=(vmem, hbm),
        scratch_shapes=[
            pltpu.VMEM((PACK, M, LANES), BF),
            pltpu.VMEM((PACK, M, LANES), BF),
            pltpu.VMEM((LW, M, LANES), BF),
            pltpu.VMEM((LV - HELD, M, 4 * C), BF),
            pltpu.SemaphoreType.DMA((7,)),
        ],
        compiler_params=params(),
        cost_estimate=cost(2_000_000_000, 4000000),
    )(pltpu.with_memory_space_constraint(near, pltpu.HBM), pltpu.with_memory_space_constraint(far, pltpu.HBM), own, mate, w_v, keep)


def mix_kernel(attn_ref, held_ref, v_in, own_ref, w_ref, out_ref, v_ref, att_ref, sems):
    copy = pltpu.make_async_copy(v_in, v_ref, sems.at[0])
    copy.start()
    lane = lax.broadcasted_iota(jnp.int32, (1, 4 * C), 1) % LANES
    masks = [(lane // (4 * HD) == h).astype(BF) for h in range(HEADS // 2)]
    lane_tiles = HEADS * M // 128
    attn = jnp.concatenate(
        [jnp.concatenate([attn_ref[a * lane_tiles + b] for b in range(lane_tiles)], axis=-1) for a in range(M // 8)],
        axis=0,
    )
    for first, ref in ((0, held_ref), (HELD, v_ref)):
        if first:
            copy.wait()
        for i in range(0, ref.shape[0], 2):
            t = first + i
            for half in range(2):
                lanes = slice(half * LANES, (half + 1) * LANES)
                v = jnp.concatenate([ref[i, :, lanes], ref[i + 1, :, lanes]], axis=-1)
                vm = jnp.concatenate([v * mask for mask in masks], axis=0)
                weights = attn[:, half * 4 * M:(half + 1) * 4 * M]
                blended = jnp.dot(weights, vm, preferred_element_type=F32).astype(BF)
                att_ref[t, :, lanes] = blended[:, :LANES]
                att_ref[t + 1, :, lanes] = blended[:, LANES:]
    step = 8
    for start in range(0, LB, step):
        total = own_ref[start + 2:start + 2 + step].astype(F32).reshape(step * M, LANES)
        for b in range(3):
            x = att_ref[start + b:start + b + step].reshape(step * M, 4 * C)
            total = total + jnp.dot(x, w_ref[b], preferred_element_type=F32)
        out_ref[start:start + step] = total.astype(BF).reshape(step, M, LANES)


def mix(attn, held, v, own, w_o):
    vmem = pl.BlockSpec(memory_space=pltpu.VMEM)
    hbm = pl.BlockSpec(memory_space=pltpu.HBM)
    return pl.pallas_call(
        mix_kernel,
        in_specs=[vmem, vmem, hbm, vmem, vmem],
        out_shape=jax.ShapeDtypeStruct((LB, M, LANES), BF),
        scratch_shapes=[
            pltpu.VMEM((LV - HELD, M, 4 * C), BF),
            pltpu.VMEM((LV, M, 4 * C), BF),
            pltpu.SemaphoreType.DMA((1,)),
        ],
        compiler_params=params(),
        cost_estimate=cost(4_000_000_000, 4000000),
    )(attn, held, pltpu.with_memory_space_constraint(v, pltpu.HBM), own, w_o)


def total_kernel(parts_ref, out_ref):
    total = parts_ref[0]
    for i in range(1, parts_ref.shape[0]):
        total = total + parts_ref[i]
    for g in range(out_ref.shape[0]):
        out_ref[g] = total


def summed(parts, copies):
    return pl.pallas_call(
        total_kernel,
        out_shape=jax.ShapeDtypeStruct((copies,) + parts.shape[1:], F32),
        compiler_params=params(),
        cost_estimate=cost(0, 300000),
    )(parts)


def softmax_kernel(scale, parts_ref, out_ref):
    total = parts_ref[0]
    for i in range(1, parts_ref.shape[0]):
        total = total + parts_ref[i]
    total = total * scale
    low = lax.broadcasted_iota(jnp.int32, total.shape, 1) < M

    def halves(reduce, x, fill):
        first = reduce(jnp.where(low, x, fill), axis=-1, keepdims=True)
        second = reduce(jnp.where(low, fill, x), axis=-1, keepdims=True)
        return jnp.where(low, first, second)

    e = jnp.exp(total - halves(jnp.max, total, -jnp.inf))
    attn = (e / halves(jnp.sum, e, 0.0)).astype(BF)
    for g in range(out_ref.shape[0]):
        out_ref[g] = attn


def softmax_of(parts, scale, copies):
    return pl.pallas_call(
        functools.partial(softmax_kernel, scale),
        out_shape=jax.ShapeDtypeStruct((copies,) + parts.shape[1:], BF),
        compiler_params=params(),
        cost_estimate=cost(0, 300000),
    )(parts)


def row_order():
    old = lax.broadcasted_iota(jnp.int32, (LANES, LANES), 0)
    new = lax.broadcasted_iota(jnp.int32, (LANES, LANES), 1)
    return (old % ROWS * C + old // ROWS == new).astype(BF)


def final_kernel(back_ref, out_hbm, cells_ref, out_ref, sems):
    members = out_ref.shape[0]
    count = LB * members
    for g in range(GROUPS):
        cells_ref[g * count:(g + 1) * count] = back_ref[g].astype(F32)
    order = row_order()
    copies = []
    for m in range(members):
        cells = cells_ref[pl.ds(m, LON, stride=members)].astype(BF)
        rows = lax.dot_general(order, cells, (((1,), (1,)), ((), ())), preferred_element_type=F32)
        out_ref[m] = rows.astype(BF).reshape(C, ROWS, LON)
        copies.append(pltpu.make_async_copy(out_ref.at[m], out_hbm.at[m], sems.at[m]))
        copies[m].start()
    for copy in copies:
        copy.wait()


def final_layout(back):
    members = back.shape[1] // LB
    shape = (members, C, ROWS, LON)
    return pl.pallas_call(
        final_kernel,
        out_shape=jax.ShapeDtypeStruct(shape, BF),
        out_specs=pl.BlockSpec(memory_space=pl.ANY),
        scratch_shapes=[
            pltpu.VMEM((LON * members, LANES), F32),
            pltpu.VMEM(shape, BF),
            pltpu.SemaphoreType.DMA((members,)),
        ],
        compiler_params=params(),
        cost_estimate=cost(0, 1600000),
    )(back)


def local(fields, w_qkv, w_out):
    members_here = fields.shape[0]
    core = lax.axis_index("core")
    place = lax.axis_index(SPACE)
    group = lax.axis_index("mem")
    places = lax.axis_size(SPACE)
    last_place = places - 1

    rows = jnp.transpose(fields, (0, 2, 1, 3)).reshape(members_here, LANES, LON)
    windows = windows_of(rows).reshape(GROUPS, LW, members_here, LANES)
    arrived = lax.all_to_all(windows, "mem", split_axis=0, concat_axis=0, tiled=True)
    own = jnp.transpose(arrived, (1, 0, 2, 3)).reshape(LW, M, LANES)
    seams = [(i, i + 1) for i in range(1, last_place, 2)]
    seams = seams + [(j, i) for i, j in seams]
    near = lax.ppermute(pack(core, own), SPACE, seams)
    mate = lax.ppermute(own, "core", [(0, 1), (1, 0)])
    far = lax.ppermute(pack(1 - core, own), SPACE, seams)
    own, w_qkv = lax.optimization_barrier((own, w_qkv))
    w_qk, w_near, w_v, w_o = place_weights(core, w_qkv, w_out)
    first, late = early_scores(mate, own, w_qk)
    part, near = late_scores(near, late, first, w_near)

    row = lax.broadcasted_iota(jnp.int32, (LV, 1, 4 * C), 2) % (4 * HD) // HD
    lon = lax.broadcasted_iota(jnp.int32, (LV, 1, 4 * C), 0)
    outside = (
        ((row == 0) & (place == 0))
        | ((row == 3) & (place == last_place))
        | ((lon == 0) & (group == 0))
        | ((lon == LV - 1) & (group == GROUPS - 1))
    )
    keep = jnp.where(outside, 0.0, 1.0).astype(F32)
    part = lax.all_to_all(part, SPACE, split_axis=0, concat_axis=0, tiled=True)
    held, v = value_maps(near, far, own, mate, w_v, keep)
    part, held, v = lax.optimization_barrier((part, held, v))
    part = lax.all_to_all(summed(part, GROUPS), "mem", split_axis=0, concat_axis=0, tiled=True)
    attn = softmax_of(part, 1.0 / math.sqrt(HD * ROWS * places * LON), places)
    attn = lax.all_to_all(attn, SPACE, split_axis=0, concat_axis=0, tiled=True)
    mixed = mix(attn, held, v, own, w_o)
    mixed = jnp.transpose(mixed.reshape(LB, GROUPS, members_here, LANES), (1, 0, 2, 3))
    back = lax.all_to_all(mixed, "mem", split_axis=0, concat_axis=0, tiled=True)
    return final_layout(back.reshape(GROUPS, LB * members_here, LANES))


def solution(mesh):
    whole = Mesh(mesh.devices.reshape(4, 4, 2, 8), ("x", "y", "core", "mem"))
    return jax.shard_map(
        local,
        mesh=whole,
        in_specs=(P("mem", None, SPACE, None), P(), P()),
        out_specs=P("mem", None, SPACE, None),
        check_vma=False,
    )
```
